32 devices in a mesh: band: 2 (over x), batch: 16 (over z, y, core).
Axes of the slice: x: 2, y: 2, z: 4, core: 2. Of those that a mesh axis runs over, the one named last changes fastest.
Arguments:
- images: bfloat16 [320, 14, 14, 384], P('batch', 'band'), may hold values from -6 to 6
- cotangent: bfloat16 [320, 14, 14, 384], P('batch', 'band'), may hold values from -6 to 6
- norm1_gain: float32 [384], replicated, may hold values from 0.5 to 1.5
- norm1_shift: float32 [384], replicated, may hold values from -1.5 to 1.5
- qkv_weight: bfloat16 [384, 1152], replicated, may hold values from -0.3125 to 0.3125
- qv_bias: float32 [2, 384], replicated, may hold values from -1.5 to 1.5
- proj_weight: bfloat16 [384, 384], replicated, may hold values from -0.875 to 0.875
- proj_bias: float32 [384], replicated, may hold values from -1.5 to 1.5
- pos_in_weight: float32 [2, 96], replicated, may hold values from -4 to 4
- pos_in_bias: float32 [96], replicated, may hold values from -2.5 to 2.5
- pos_norm1_gain: float32 [96], replicated, may hold values from 0.5 to 1.5
- pos_norm1_shift: float32 [96], replicated, may hold values from -1.5 to 1.5
- pos_weight1: float32 [96, 96], replicated, may hold values from -0.625 to 0.625
- pos_bias1: float32 [96], replicated, may hold values from -1.5 to 1.5
- pos_norm2_gain: float32 [96], replicated, may hold values from 0.5 to 1.5
- pos_norm2_shift: float32 [96], replicated, may hold values from -1.5 to 1.5
- pos_weight2: float32 [96, 96], replicated, may hold values from -0.625 to 0.625
- pos_bias2: float32 [96], replicated, may hold values from -1.5 to 1.5
- pos_norm3_gain: float32 [96], replicated, may hold values from 0.5 to 1.5
- pos_norm3_shift: float32 [96], replicated, may hold values from -1.5 to 1.5
- pos_weight3: float32 [96, 12], replicated, may hold values from -1.25 to 1.25
- norm2_gain: float32 [384], replicated, may hold values from 0.5 to 1.5
- norm2_shift: float32 [384], replicated, may hold values from -1.5 to 1.5
- fc1_weight: bfloat16 [384, 1536], replicated, may hold values from -0.3125 to 0.3125
- fc1_bias: float32 [1536], replicated, may hold values from -1.5 to 1.5
- fc2_weight: bfloat16 [1536, 384], replicated, may hold values from -0.15625 to 0.15625
- fc2_bias: float32 [384], replicated, may hold values from -1.5 to 1.5
Outputs:
- out_images: bfloat16 [320, 14, 14, 384], P('batch', 'band')
- grad_images: float32 [320, 14, 14, 384], P('batch', 'band')
- grad_norm1_gain: float32 [384], replicated
- grad_norm1_shift: float32 [384], replicated
- grad_qkv_weight: float32 [384, 1152], replicated
- grad_qv_bias: float32 [2, 384], replicated
- grad_proj_weight: float32 [384, 384], replicated
- grad_proj_bias: float32 [384], replicated
- grad_pos_in_weight: float32 [2, 96], replicated
- grad_pos_in_bias: float32 [96], replicated
- grad_pos_norm1_gain: float32 [96], replicated
- grad_pos_norm1_shift: float32 [96], replicated
- grad_pos_weight1: float32 [96, 96], replicated
- grad_pos_bias1: float32 [96], replicated
- grad_pos_norm2_gain: float32 [96], replicated
- grad_pos_norm2_shift: float32 [96], replicated
- grad_pos_weight2: float32 [96, 96], replicated
- grad_pos_bias2: float32 [96], replicated
- grad_pos_norm3_gain: float32 [96], replicated
- grad_pos_norm3_shift: float32 [96], replicated
- grad_pos_weight3: float32 [96, 12], replicated
- grad_norm2_gain: float32 [384], replicated
- grad_norm2_shift: float32 [384], replicated
- grad_fc1_weight: float32 [384, 1536], replicated
- grad_fc1_bias: float32 [1536], replicated
- grad_fc2_weight: float32 [1536, 384], replicated
- grad_fc2_bias: float32 [384], replicated
The draws below stay inside these ranges and needn't reach their ends.
All inputs are finite; a program needn't handle non-finite values.
Results may differ from the reference program's by a relative error of at most 0.018.
Values may be sent and summed in bfloat16 or wider, within the bound.
No kernel may reach another device: no remote copies, remote signals or barrier semaphores. Data moves between devices by JAX's collectives and lax.ppermute only.
A program may use at most 192 MiB of HBM per device.

```python
import jax
import jax.numpy as jnp
from jax import lax

C = 384
HEADS = 12
FF = 1536
POS = 96
GROUP = 7
IMG_DEV = 20
HEAD_DIM = 32
SIDE = 14
IMAGES = 320
N_BATCH = 16


def draw_cotangent(key, part):
    key = jax.random.fold_in(key, 11)
    ramp = (jnp.arange(IMAGES, dtype=jnp.float32) / IMAGES).reshape(IMAGES, 1, 1, 1)
    entries = jax.random.truncated_normal(key, -4.0, 4.0, (IMAGES, SIDE, SIDE, C), jnp.float32)
    result = entries * (0.5 + ramp)
    return result.astype(jnp.bfloat16)


def level_of(stream_key, dims, split, smallest, top_value):
    gain, own = 1.0, jax.random.fold_in(stream_key, 6)
    for dim, shards_of in split:
        draws = jnp.exp(jax.random.uniform(jax.random.fold_in(own, dim), (shards_of,), jnp.float32, smallest / len(split), top_value / len(split)))
        gain = gain * jnp.repeat(draws, dims[dim] // shards_of).reshape([-1 if axis == dim else 1 for axis in range(len(dims))])
    return gain


def normal_values(rng, extent, deviation, most, shards=(), kind=jnp.bfloat16):
    array = jax.random.normal(rng, extent, jnp.float32) * deviation
    if len(shards) > 0:
        array = level_of(rng, extent, shards, -0.22, 0.18) * array
    return jnp.clip(array, min=-most, max=most).astype(kind)


def setup_inputs(seed: int = 0) -> dict:
    seeds = jax.random.split(jax.random.key(seed), 28)
    images = normal_values(seeds[0], (IMAGES, SIDE, SIDE, C), 1.0, 6.0, ((0, 16), (1, 2)))
    cotangent = draw_cotangent(jax.random.fold_in(seeds[27], 71), 0)
    norm1_gain = jnp.clip(1.0 + 0.1 * jax.random.normal(seeds[2], (C,), jnp.float32), 0.5, 1.5)
    norm1_shift = normal_values(seeds[3], (C,), 0.3, 1.5, (), jnp.float32)
    qkv_weight = normal_values(seeds[4], (C, 3 * C), C ** -0.5, 0.3125)
    qv_bias = normal_values(seeds[5], (2, C), 0.3, 1.5, (), jnp.float32)
    proj_weight = normal_values(seeds[6], (C, C), (C // 8) ** -0.5, 0.875)
    proj_bias = normal_values(seeds[7], (C,), 0.3, 1.5, (), jnp.float32)
    pos_in_weight = normal_values(seeds[8], (2, POS), 2 ** -0.5, 4.0, (), jnp.float32)
    pos_in_bias = normal_values(seeds[9], (POS,), 0.5, 2.5, (), jnp.float32)
    pos_norm1_gain = jnp.clip(1.0 + 0.1 * jax.random.normal(seeds[10], (POS,), jnp.float32), 0.5, 1.5)
    pos_norm1_shift = normal_values(seeds[11], (POS,), 0.3, 1.5, (), jnp.float32)
    pos_weight1 = normal_values(seeds[12], (POS, POS), POS ** -0.5, 0.625, (), jnp.float32)
    pos_bias1 = normal_values(seeds[13], (POS,), 0.3, 1.5, (), jnp.float32)
    pos_norm2_gain = jnp.clip(1.0 + 0.1 * jax.random.normal(seeds[14], (POS,), jnp.float32), 0.5, 1.5)
    pos_norm2_shift = normal_values(seeds[15], (POS,), 0.3, 1.5, (), jnp.float32)
    pos_weight2 = normal_values(seeds[16], (POS, POS), POS ** -0.5, 0.625, (), jnp.float32)
    pos_bias2 = normal_values(seeds[17], (POS,), 0.3, 1.5, (), jnp.float32)
    pos_norm3_gain = jnp.clip(1.0 + 0.1 * jax.random.normal(seeds[18], (POS,), jnp.float32), 0.5, 1.5)
    pos_norm3_shift = normal_values(seeds[19], (POS,), 0.3, 1.5, (), jnp.float32)
    pos_weight3 = normal_values(seeds[20], (POS, HEADS), (POS // 4) ** -0.5, 1.25, (), jnp.float32)
    norm2_gain = jnp.clip(1.0 + 0.1 * jax.random.normal(seeds[21], (C,), jnp.float32), 0.5, 1.5)
    norm2_shift = normal_values(seeds[22], (C,), 0.3, 1.5, (), jnp.float32)
    fc1_weight = normal_values(seeds[23], (C, FF), C ** -0.5, 0.3125)
    fc1_bias = normal_values(seeds[24], (FF,), 0.3, 1.5, (), jnp.float32)
    fc2_weight = normal_values(seeds[25], (FF, C), FF ** -0.5, 0.15625)
    fc2_bias = normal_values(seeds[26], (C,), 0.3, 1.5, (), jnp.float32)
    return {"images": images, "cotangent": cotangent, "norm1_gain": norm1_gain, "norm1_shift": norm1_shift, "qkv_weight": qkv_weight, "qv_bias": qv_bias, "proj_weight": proj_weight, "proj_bias": proj_bias, "pos_in_weight": pos_in_weight, "pos_in_bias": pos_in_bias, "pos_norm1_gain": pos_norm1_gain, "pos_norm1_shift": pos_norm1_shift, "pos_weight1": pos_weight1, "pos_bias1": pos_bias1, "pos_norm2_gain": pos_norm2_gain, "pos_norm2_shift": pos_norm2_shift, "pos_weight2": pos_weight2, "pos_bias2": pos_bias2, "pos_norm3_gain": pos_norm3_gain, "pos_norm3_shift": pos_norm3_shift, "pos_weight3": pos_weight3, "norm2_gain": norm2_gain, "norm2_shift": norm2_shift, "fc1_weight": fc1_weight, "fc1_bias": fc1_bias, "fc2_weight": fc2_weight, "fc2_bias": fc2_bias}


@jax.custom_vjp
def low(v):
    return lax.optimization_barrier(v.astype(jnp.bfloat16)).astype(jnp.float32)

@jax.custom_vjp
def low_back(v):
    return v

def low_keep(v):
    return (low(v), None)

def low_pass(kept, grad):
    return (grad,)

def back_keep(v):
    return (v, None)

def back_low(kept, grad):
    return (low(grad),)
low.defvjp(low_keep, low_pass)
low_back.defvjp(back_keep, back_low)
HIGH = lax.Precision.HIGHEST
EPSILON = 1e-05

def layer_norm(values, norm_gain, norm_shift):
    centred = values - lax.optimization_barrier(jnp.mean(values, axis=-1, keepdims=True))
    variance = lax.optimization_barrier(jnp.mean(centred * centred, axis=-1, keepdims=True))
    return centred * lax.rsqrt(variance + EPSILON) * norm_gain + norm_shift

def pair_index():
    cells = jnp.arange(GROUP * GROUP, dtype=jnp.int32)
    cell_rows = cells // GROUP
    cell_cols = cells % GROUP
    return (cell_rows[:, None] - cell_rows[None, :] + GROUP - 1) * (2 * GROUP - 1) + cell_cols[:, None] - cell_cols[None, :] + GROUP - 1

def position_table(in_weight, in_bias, gain_one, shift_one, weight_one, bias_one, gain_two, shift_two, weight_two, bias_two, gain_three, shift_three, weight_three):
    offsets = jnp.arange((2 * GROUP - 1) * (2 * GROUP - 1), dtype=jnp.int32)
    coords = jnp.stack([offsets // (2 * GROUP - 1) - (GROUP - 1), offsets % (2 * GROUP - 1) - (GROUP - 1)], axis=1).astype(jnp.float32)
    hidden = jnp.dot(coords, in_weight, precision=HIGH) + in_bias
    hidden = jnp.dot(jax.nn.gelu(layer_norm(hidden, gain_one, shift_one), approximate=False), weight_one, precision=HIGH) + bias_one
    hidden = jnp.dot(jax.nn.gelu(layer_norm(hidden, gain_two, shift_two), approximate=False), weight_two, precision=HIGH) + bias_two
    return jnp.dot(jax.nn.gelu(layer_norm(hidden, gain_three, shift_three), approximate=False), weight_three, precision=HIGH)

def forward(params, block):
    norm1_gain, norm1_shift, qkv_weight, qv_bias, proj_weight, proj_bias, pos_in_weight, pos_in_bias, pos_norm1_gain, pos_norm1_shift, pos_weight1, pos_bias1, pos_norm2_gain, pos_norm2_shift, pos_weight2, pos_bias2, pos_norm3_gain, pos_norm3_shift, pos_weight3, norm2_gain, norm2_shift, fc1_weight, fc1_bias, fc2_weight, fc2_bias = params
    img_count = block.shape[0]
    normed = low_back(low(layer_norm(block, norm1_gain, norm1_shift)))
    grouped = normed.reshape(img_count, GROUP, 2, GROUP, 2, C).transpose(0, 2, 4, 1, 3, 5)
    grouped = grouped.reshape(img_count * 4, GROUP * GROUP, C)
    projected = jnp.dot(grouped, qkv_weight, precision=HIGH)
    queries = low_back(low(projected[:, :, :C] + qv_bias[0]))
    key_vectors = low_back(low(projected[:, :, C:2 * C]))
    val_vectors = low_back(low(projected[:, :, 2 * C:] + qv_bias[1]))
    head_shape = (img_count * 4, GROUP * GROUP, HEADS, HEAD_DIM)
    table = position_table(pos_in_weight, pos_in_bias, pos_norm1_gain, pos_norm1_shift, pos_weight1, pos_bias1, pos_norm2_gain, pos_norm2_shift, pos_weight2, pos_bias2, pos_norm3_gain, pos_norm3_shift, pos_weight3)
    bias_heads = table[pair_index()].transpose(2, 0, 1)
    scores = jnp.einsum('gihd,gjhd->ghij', queries.reshape(head_shape), key_vectors.reshape(head_shape), precision=HIGH)
    scores = low_back(HEAD_DIM ** (-0.5) * scores + bias_heads)
    probs = low(jax.nn.softmax(scores, axis=-1))
    attended = jnp.einsum('ghij,gjhd->gihd', probs, val_vectors.reshape(head_shape), precision=HIGH)
    attended = low_back(low(attended.reshape(img_count * 4, GROUP * GROUP, C)))
    attended = attended.reshape(img_count, 2, 2, GROUP, GROUP, C).transpose(0, 3, 1, 4, 2, 5).reshape(img_count, SIDE, SIDE, C)
    middle = block + low_back(jnp.dot(attended, proj_weight, precision=HIGH) + proj_bias)
    normed2 = low_back(low(layer_norm(middle, norm2_gain, norm2_shift)))
    pre_act = low_back(jnp.dot(normed2, fc1_weight, precision=HIGH) + fc1_bias)
    activ = low(jax.nn.gelu(pre_act, approximate=False))
    return middle + low_back(jnp.dot(activ, fc2_weight, precision=HIGH) + fc2_bias)

def reference(images, cotangent, norm1_gain, norm1_shift, qkv_weight, qv_bias, proj_weight, proj_bias, pos_in_weight, pos_in_bias, pos_norm1_gain, pos_norm1_shift, pos_weight1, pos_bias1, pos_norm2_gain, pos_norm2_shift, pos_weight2, pos_bias2, pos_norm3_gain, pos_norm3_shift, pos_weight3, norm2_gain, norm2_shift, fc1_weight, fc1_bias, fc2_weight, fc2_bias):
    params = tuple((item.astype(jnp.float32) for item in (norm1_gain, norm1_shift, qkv_weight, qv_bias, proj_weight, proj_bias, pos_in_weight, pos_in_bias, pos_norm1_gain, pos_norm1_shift, pos_weight1, pos_bias1, pos_norm2_gain, pos_norm2_shift, pos_weight2, pos_bias2, pos_norm3_gain, pos_norm3_shift, pos_weight3, norm2_gain, norm2_shift, fc1_weight, fc1_bias, fc2_weight, fc2_bias)))
    image_blocks = images.astype(jnp.float32).reshape(N_BATCH, IMG_DEV, SIDE, SIDE, C)
    cot_blocks = cotangent.astype(jnp.float32).reshape(N_BATCH, IMG_DEV, SIDE, SIDE, C)

    def one_block(totals, block_pair):
        block, block_cot = block_pair
        outputs, pull = jax.vjp(forward, params, block)
        grad_set, image_grad = pull(block_cot)
        totals = jax.tree.map(jnp.add, totals, grad_set)
        return (totals, (outputs.astype(jnp.bfloat16), image_grad))
    zero_set = jax.tree.map(jnp.zeros_like, params)
    totals, (out_blocks, grad_blocks) = lax.scan(one_block, zero_set, (image_blocks, cot_blocks))
    out_images = out_blocks.reshape(IMAGES, SIDE, SIDE, C)
    grad_images = grad_blocks.reshape(IMAGES, SIDE, SIDE, C)
    return (out_images, grad_images, totals[0], totals[1], totals[2], totals[3], totals[4], totals[5], totals[6], totals[7], totals[8], totals[9], totals[10], totals[11], totals[12], totals[13], totals[14], totals[15], totals[16], totals[17], totals[18], totals[19], totals[20], totals[21], totals[22], totals[23], totals[24])
```

```python
import math
from functools import partial

import jax
import jax.numpy as jnp
import numpy as np
from jax import lax
from jax.experimental import pallas as pl
from jax.experimental.pallas import tpu as pltpu
from jax.sharding import PartitionSpec as P

HEADS = 12
GROUP = 7
HEAD_DIM = 32
SPAN = 2 * GROUP - 1
HIGH = lax.Precision.HIGHEST
EPSILON = 1e-05
SCALE = HEAD_DIM**-0.5
MASKED = -1e30
PAD_COLS = 16
TOKENS = GROUP * PAD_COLS
LANES = 128
PER_BLOCK = LANES // HEAD_DIM
STACK = PER_BLOCK * TOKENS
KEPT = (GROUP + 1) // 2
SENT = GROUP - KEPT
OFFSETS = 176
WIDE = SPAN * PAD_COLS
F32 = jnp.float32
BF16 = jnp.bfloat16


def dot(a, b, precision=None):
    return lax.dot_general(a, b, (((1,), (0,)), ((), ())), precision=precision, preferred_element_type=F32)


def dot_nt(a, b, precision=None):
    return lax.dot_general(a, b, (((1,), (1,)), ((), ())), precision=precision, preferred_element_type=F32)


def dot_tn(a, b, precision=None):
    return lax.dot_general(a, b, (((0,), (0,)), ((), ())), precision=precision, preferred_element_type=F32)


def whole(shape):
    zeros = (0,) * len(shape)
    return pl.BlockSpec(shape, lambda *_: zeros, pipeline_mode=pl.Buffered(1))


def normalise(values):
    mean = jnp.mean(values, axis=-1, keepdims=True)
    centred = values - mean
    inverse = lax.rsqrt(jnp.mean(centred * centred, axis=-1, keepdims=True) + EPSILON)
    return centred * inverse, inverse


def normalise_back(grad_hat, hat, inverse):
    first = jnp.mean(grad_hat, axis=-1, keepdims=True)
    second = jnp.mean(grad_hat * hat, axis=-1, keepdims=True)
    return inverse * (grad_hat - first - hat * second)


def gelu_both(v):
    cdf = 0.5 + 0.5 * lax.erf(v * (0.5**0.5))
    density = jnp.exp(-0.5 * v * v) * ((2.0 * np.pi) ** -0.5)
    return v * cdf, cdf + v * density


def column_sum(values):
    return jnp.sum(values, axis=0, keepdims=True)


SMALL = 24


def launch(kernel, name, grid, inputs, in_specs, out_shape, out_specs, so_far=(), scratch=(), flops=0,
           after=(), vmem=16, through=()):
    count, held = len(inputs), len(so_far) + len(after) + len(through)
    own = len(out_shape)
    hand = {count + len(so_far) + len(after) + i: own + i for i in range(len(through))}
    inner = kernel
    if held:
        kernel = lambda *refs: inner(
            *refs[:count], *refs[count + held : count + held + own], *refs[count + held + own + len(through) :]
        )
    moved = sum(a.size * a.dtype.itemsize for a in (*inputs, *out_shape))
    return pl.pallas_call(
        kernel,
        grid=grid,
        in_specs=list(in_specs) + [pl.BlockSpec(memory_space=pl.ANY)] * held,
        out_specs=list(out_specs) + [pl.BlockSpec(memory_space=pl.ANY)] * len(through),
        out_shape=list(out_shape) + [shaped(a.shape, a.dtype) for a in through],
        input_output_aliases={count + i: i for i in range(len(so_far))} | hand,
        scratch_shapes=list(scratch),
        compiler_params=pltpu.CompilerParams(vmem_limit_bytes=vmem * 2**20),
        cost_estimate=pl.CostEstimate(flops=int(flops), bytes_accessed=int(moved), transcendentals=0),
        name=name,
    )(*inputs, *so_far, *after, *through)


def small_launch(kernel, name, inputs, out_shape, scratch=(), flops=0, after=(), vmem=16, through=()):
    specs = [pl.BlockSpec(memory_space=pltpu.SMEM if a.dtype == jnp.int32 else pltpu.VMEM) for a in inputs]
    outs = [pl.BlockSpec(memory_space=pltpu.VMEM)] * len(out_shape)
    return launch(kernel, name, (), inputs, specs, out_shape, outs, scratch=scratch, flops=flops, after=after, vmem=vmem,
                  through=through)


def shaped(shape, dtype):
    return jax.ShapeDtypeStruct(shape, dtype)


FEED_PART = 512
TOKEN = shaped((8, LANES), F32)


def token_kernel(token):
    token[...] = jnp.zeros_like(token)


def merge_kernel(source, target, token):
    target[...] = source[...].astype(target.dtype)
    token[...] = jnp.zeros_like(token)


def pack_kernel(pieces, *refs):
    count = 1 + max(piece[0] for piece in pieces)
    sources, outs, (token, sems) = refs[:count], refs[count:-2], refs[-2:]
    token[...] = jnp.zeros_like(token)
    copies = []
    for (source, first, images), out in zip(pieces, outs):
        for row in range(SENT):
            copies.append(
                pltpu.make_async_copy(
                    sources[source].at[first : first + images, 2 * row + 1], out.at[:, row], sems.at[len(copies)]
                )
            )
    for copy in copies:
        copy.start()
    for copy in copies:
        copy.wait()


def pack_rows(sources, pieces, after=()):
    _, _, cols, width = sources[0].shape
    vector = pl.BlockSpec(memory_space=pltpu.VMEM)
    return launch(
        partial(pack_kernel, pieces),
        "pack_rows",
        (),
        sources,
        [pl.BlockSpec(memory_space=pl.ANY)] * len(sources),
        [shaped((count, SENT, cols, width), BF16) for _, _, count in pieces] + [TOKEN],
        [vector] * (len(pieces) + 1),
        scratch=[pltpu.SemaphoreType.DMA((SENT * len(pieces),))],
        after=after,
        vmem=60,
    )


def merge_rows(received, target, first):
    count, _, cols, width = received.shape
    unit = math.gcd(first, count)
    begin = first // unit
    return launch(
        merge_kernel,
        "merge_rows",
        (count // unit, SENT),
        (received,),
        [pl.BlockSpec((unit, 1, cols, width), lambda i, r: (i, r, 0, 0))],
        [shaped(target.shape, target.dtype), TOKEN],
        [pl.BlockSpec((unit, 1, cols, width), lambda i, r: (i + begin, 2 * r + 1, 0, 0)), whole(TOKEN.shape)],
        so_far=(target,),
    )


def position_layers(refs):
    (in_w, in_b, g1, s1, w1, b1, g2, s2, w2, b2, g3, s3, _) = refs
    width = in_w.shape[1]
    offset = lax.broadcasted_iota(jnp.int32, (OFFSETS, width), 0)
    rows = (offset // SPAN - (GROUP - 1)).astype(F32)
    cols = (offset % SPAN - (GROUP - 1)).astype(F32)
    hidden = rows * in_w[0:1, :] + cols * in_w[1:2, :] + in_b[...][None, :]
    kept = []
    for gain, shift, weight, bias in ((g1, s1, w1, b1), (g2, s2, w2, b2), (g3, s3, None, None)):
        hat, inverse = normalise(hidden)
        active, slope = gelu_both(hat * gain[...][None, :] + shift[...][None, :])
        kept.append((hat, inverse, active, slope))
        if weight is not None:
            hidden = dot(active, weight[...], HIGH) + bias[...][None, :]
    return rows, cols, kept


def pick_offsets(place):
    offset = lax.broadcasted_iota(jnp.int32, (OFFSETS, WIDE), 0)
    lane = lax.broadcasted_iota(jnp.int32, (OFFSETS, WIDE), 1)
    wanted = lane // PAD_COLS * SPAN + lane % PAD_COLS // 2 - place + GROUP - 1
    return jnp.where(offset == wanted, 1.0, 0.0).astype(F32)


def bias_kernel(*refs):
    ins, (out, strip) = refs[:13], refs[13:]
    _, _, kept = position_layers(ins)
    table = dot_nt(ins[12][...], kept[2][2], HIGH)
    lane = lax.broadcasted_iota(jnp.int32, (HEADS, WIDE), 1)
    even = lane % 2 == 0
    strip[...] = jnp.full(strip.shape, MASKED, F32)
    for place in range(GROUP):
        spread = dot(table, pick_offsets(place), HIGH)
        strip[:, 2 * place, 0:WIDE] = jnp.where(even, spread, MASKED)
        strip[:, 2 * place + 1, 0:WIDE] = jnp.where(even, MASKED, spread)
    for row in range(GROUP):
        start = (GROUP - 1 - row) * PAD_COLS
        out[:, row * PAD_COLS : (row + 1) * PAD_COLS, :] = strip[:, :, start : start + TOKENS]


def pair_bias(pos, through):
    return small_launch(
        bias_kernel,
        "pair_bias",
        pos,
        [shaped((HEADS, TOKENS, TOKENS), F32)],
        [pltpu.VMEM((HEADS, PAD_COLS, 2 * LANES), F32)],
        through=through,
        vmem=60,
    )


def put_pair(ref, start, values):
    high = values.astype(BF16)
    ref[start : start + SMALL, :] = high
    ref[start + SMALL : start + 2 * SMALL, :] = (values - high.astype(F32)).astype(BF16)


def get_pair(ref, start):
    return ref[start : start + SMALL, :].astype(F32) + ref[start + SMALL : start + 2 * SMALL, :].astype(F32)


def gather_small_kernel(feed_small, feed_b1, att_small, norm_small, grad_pair, out, small):
    width = feed_small.shape[1]
    strip = jnp.zeros((HEADS, PAD_COLS, WIDE), F32)
    for row in range(GROUP):
        start = (GROUP - 1 - row) * PAD_COLS
        piece = grad_pair[:, row * PAD_COLS : (row + 1) * PAD_COLS, :]
        strip = strip + jnp.pad(piece, ((0, 0), (0, 0), (start, WIDE - start - TOKENS)))
    table = jnp.zeros((HEADS, OFFSETS), F32)
    for place in range(GROUP):
        folded = strip[:, 2 * place, :] + strip[:, 2 * place + 1, :]
        table = table + dot_nt(folded, pick_offsets(place), HIGH)
    small[...] = jnp.zeros_like(small)
    small[0:4, :] = feed_small[0:4, :]
    small[4:6, :] = norm_small[0:2, :]
    small[6:8, :] = att_small[0:2, :]
    for part in range(feed_b1.shape[1] // width):
        small[8 + part : 9 + part, :] = feed_b1[:, part * width : (part + 1) * width]
    small[12 : 12 + HEADS, 0:OFFSETS] = table
    put_pair(out, 0, small[...])


def gather_small(feed_small, feed_b1, att_small, norm_small, grad_pair):
    width = feed_small.shape[1]
    return small_launch(
        gather_small_kernel,
        "gather_small",
        (feed_small, feed_b1, att_small, norm_small, grad_pair.reshape(HEADS, TOKENS, TOKENS)),
        [shaped((2 * SMALL, width), BF16)],
        [pltpu.VMEM((SMALL, width), F32)],
    )[0]


def finish_small_kernel(*refs):
    ins, small, outs = refs[:13], refs[13], refs[14:]
    (in_w, in_b, g1, s1, w1, b1, g2, s2, w2, b2, g3, s3, w3) = ins
    (o_n1_gain, o_n1_shift, o_qv, o_proj_b, o_n2_gain, o_n2_shift, o_fc1_b, o_fc2_b) = outs[:8]
    (o_in_w, o_in_b, o_g1, o_s1, o_w1, o_b1, o_g2, o_s2, o_w2, o_b2, o_g3, o_s3, o_w3) = outs[8:]
    o_n2_gain[...] = small[0, :]
    o_n2_shift[...] = small[1, :]
    o_fc2_b[...] = small[2, :]
    o_proj_b[...] = small[3, :]
    o_n1_gain[...] = small[4, :]
    o_n1_shift[...] = small[5, :]
    o_qv[...] = small[6:8, :]
    width = small.shape[1]
    for part in range(o_fc1_b.shape[0] // width):
        o_fc1_b[part * width : (part + 1) * width] = small[8 + part, :]
    rows, cols, kept = position_layers(ins)
    table = small[12 : 12 + HEADS, 0:OFFSETS]
    o_w3[...] = dot(table, kept[2][2], HIGH)
    grad_active = dot(table.T, w3[...], HIGH)
    stages = (
        (g3, o_g3, o_s3, o_b2, o_w2, w2),
        (g2, o_g2, o_s2, o_b1, o_w1, w1),
        (g1, o_g1, o_s1, o_in_b, None, None),
    )
    for level, (gain, o_gain, o_shift, o_bias, o_weight, weight) in zip((2, 1, 0), stages):
        hat, inverse, _, slope = kept[level]
        grad_norm = grad_active * slope
        o_gain[...] = jnp.sum(grad_norm * hat, axis=0)
        o_shift[...] = jnp.sum(grad_norm, axis=0)
        grad_hidden = normalise_back(grad_norm * gain[...][None, :], hat, inverse)
        o_bias[...] = jnp.sum(grad_hidden, axis=0)
        if weight is not None:
            o_weight[...] = dot(kept[level - 1][2].T, grad_hidden, HIGH)
            grad_active = dot_nt(grad_hidden, weight[...], HIGH)
        else:
            o_in_w[0:1, :] = column_sum(grad_hidden * rows)
            o_in_w[1:2, :] = column_sum(grad_hidden * cols)


def finish_small(pos, small, hidden):
    width = small.shape[1]
    shapes = [(width,), (width,), (2, width), (width,), (width,), (width,), (hidden,), (width,)]
    return small_launch(
        finish_small_kernel,
        "finish_small",
        (*pos, small),
        [shaped(s, F32) for s in shapes] + [shaped(p.shape, F32) for p in pos],
    )


def stack_heads(block, mask):
    return jnp.concatenate([block] * PER_BLOCK, axis=0) * mask


def place_rows(band, kept_ref, received_ref, padded):
    upper = band * SENT
    lower = (1 - band) * KEPT
    for row in range(KEPT):
        padded[:, row + upper, 0 : 2 * GROUP, :] = kept_ref[:, 2 * row]
    for row in range(SENT):
        padded[:, row + lower, 0 : 2 * GROUP, :] = received_ref[:, row]


def return_rows(band, placed, kept_ref, sent_ref):
    upper = band * SENT
    lower = (1 - band) * KEPT
    for row in range(KEPT):
        kept_ref[:, 2 * row] = placed[:, row + upper, 0 : 2 * GROUP, :]
    for row in range(SENT):
        sent_ref[:, row] = placed[:, row + lower, 0 : 2 * GROUP, :].astype(sent_ref.dtype)


def attend_kernel(count, where, images, received, gain, shift, weight, bias, pair, mask,
                  x_out, normed_out, qkv_out, probs_out, att_out, padded):
    width = images.shape[3]

    @pl.when(pl.program_id(0) == 0)
    def _():
        padded[...] = jnp.zeros_like(padded)

    place_rows(where[0], images, received, padded)
    x = padded[...].reshape(count * TOKENS, width)
    x_out[...] = x
    hat, _ = normalise(x.astype(F32))
    normed = (hat * gain[...][None, :] + shift[...][None, :]).astype(BF16)
    normed_out[...] = normed
    piece = dot(normed, weight[...])
    qkv_out[:, 0:width] = (piece[:, 0:width] + bias[0:1, :]).astype(BF16)
    qkv_out[:, width : 2 * width] = piece[:, width : 2 * width].astype(BF16)
    qkv_out[:, 2 * width :] = (piece[:, 2 * width :] + bias[1:2, :]).astype(BF16)
    masks = mask[...]
    for image in range(count):
        rows = slice(image * TOKENS, (image + 1) * TOKENS)
        for block in range(HEADS // PER_BLOCK):
            at = block * LANES
            query = qkv_out[rows, at : at + LANES]
            keys = stack_heads(qkv_out[rows, width + at : width + at + LANES], masks)
            vals = stack_heads(qkv_out[rows, 2 * width + at : 2 * width + at + LANES], masks)
            here = slice(block * STACK, (block + 1) * STACK)
            scores = dot_nt(keys, query) * SCALE + pair[here, :]
            scores = scores.reshape(PER_BLOCK, TOKENS, TOKENS)
            probs = jnp.exp(scores - jnp.max(scores, axis=1, keepdims=True))
            probs = probs * (1.0 / jnp.sum(probs, axis=1, keepdims=True))
            probs = probs.astype(BF16).reshape(STACK, TOKENS)
            probs_out[image, here, :] = probs
            att_out[rows, at : at + LANES] = dot_tn(probs, vals).astype(BF16)


def attend(where, images, received, first, per_step, gain, shift, weight, bias, pair, mask, so_far, through):
    total, _, cols, width = images.shape
    count = received.shape[0]
    begin = first // per_step
    rows = per_step * TOKENS
    row_spec = lambda w: pl.BlockSpec((rows, w), lambda i: (i + begin, 0))
    fixed = (gain, shift, weight, bias, pair.reshape(HEADS * TOKENS, TOKENS), mask)
    return launch(
        partial(attend_kernel, per_step),
        "attend",
        (count // per_step,),
        (where, images, received, *fixed),
        [
            pl.BlockSpec(memory_space=pltpu.SMEM),
            pl.BlockSpec((per_step, GROUP, cols, width), lambda i: (i + begin, 0, 0, 0)),
            pl.BlockSpec((per_step, SENT, cols, width), lambda i: (i, 0, 0, 0)),
        ]
        + [whole(a.shape) for a in fixed],
        [
            shaped((total * TOKENS, width), BF16),
            shaped((total * TOKENS, width), BF16),
            shaped((total * TOKENS, 3 * width), BF16),
            shaped((total, HEADS * TOKENS, TOKENS), BF16),
            shaped((total * TOKENS, width), BF16),
        ],
        [
            row_spec(width),
            row_spec(width),
            row_spec(3 * width),
            pl.BlockSpec((per_step, HEADS * TOKENS, TOKENS), lambda i: (i + begin, 0, 0)),
            row_spec(width),
        ],
        so_far=so_far,
        scratch=[pltpu.VMEM((per_step, GROUP, PAD_COLS, width), BF16)],
        flops=count * TOKENS * width * width * 12,
        through=through,
        vmem=60,
    )


def feed_kernel(count, where, cot, received, x_ref, att_ref, proj_w, proj_b, gain, shift, w1, b1, w2, b2,
                out_kept, grad_mid, grad_att, out_send, o_small, o_b1, o_first, o_second, a_proj,
                padded, placed, pair):
    width = x_ref.shape[1]
    hidden = w1.shape[1]
    step = pl.program_id(0)

    @pl.when(step == 0)
    def _():
        for ref in (padded, o_small, o_b1, pair, a_proj):
            ref[...] = jnp.zeros_like(ref)

    place_rows(where[0], cot, received, padded)
    up = padded[...].reshape(count * TOKENS, width)
    up_f = up.astype(F32)
    up_turned = up.T
    att = att_ref[...]
    middle = x_ref[...].astype(F32) + (dot(att, proj_w[...]) + proj_b[...][None, :])
    hat, inverse = normalise(middle)
    normed = (hat * gain[...][None, :] + shift[...][None, :]).astype(BF16)
    normed_turned = normed.T
    result = middle + b2[...][None, :]
    grad_normed = jnp.zeros((count * TOKENS, width), F32)
    for start in range(0, hidden, FEED_PART):
        cols = slice(start, start + FEED_PART)
        active, slope = gelu_both(dot(normed, w1[:, cols]) + b1[cols][None, :])
        active = active.astype(BF16)
        result = result + dot(active, w2[cols, :])
        grad_pre = (dot_nt(up, w2[cols, :]) * slope).astype(BF16)
        grad_normed = grad_normed + dot_nt(grad_pre, w1[:, cols])
        pair[0, :, cols] += dot(normed_turned, grad_pre)
        pair[1, :, cols] += dot(up_turned, active)
        o_b1[:, cols] += column_sum(grad_pre.astype(F32))
    placed[...] = result.astype(BF16).reshape(placed.shape)
    return_rows(where[0], placed, out_kept, out_send)
    grad_normed = grad_normed.astype(BF16).astype(F32)
    grad_middle = up_f + normalise_back(grad_normed * gain[...][None, :], hat, inverse)
    grad_mid[...] = grad_middle
    branch = grad_middle.astype(BF16)
    a_proj[...] += dot(att.T, branch)
    grad_att[...] = dot_nt(branch, proj_w[...]).astype(BF16)
    o_small[0:1, :] += column_sum(grad_normed * hat)
    o_small[1:2, :] += column_sum(grad_normed)
    o_small[2:3, :] += column_sum(up_f)
    o_small[3:4, :] += column_sum(branch.astype(F32))

    @pl.when(step == pl.num_programs(0) - 1)
    def _():
        core = where[1]
        for part in range(hidden // width):
            cols = slice(part * width, (part + 1) * width)
            o_first[part] = pair[core, :, cols].astype(BF16)
            o_second[part] = pair[1 - core, :, cols].astype(BF16)


def feed(where, cotangent, received, per_step, x, att, weights):
    total, _, cols, width = cotangent.shape
    hidden = weights[4].shape[1]
    rows = per_step * TOKENS
    row_spec = lambda w: pl.BlockSpec((rows, w), lambda i: (i, 0))
    image_spec = lambda n: pl.BlockSpec((per_step, n, cols, width), lambda i: (i, 0, 0, 0))
    accumulated = [
        shaped((8, width), F32),
        shaped((1, hidden), F32),
        shaped((hidden // width, width, width), BF16),
        shaped((hidden // width, width, width), BF16),
        shaped((width, width), F32),
    ]
    return launch(
        partial(feed_kernel, per_step),
        "feed",
        (total // per_step,),
        (where, cotangent, received, x, att, *weights),
        [pl.BlockSpec(memory_space=pltpu.SMEM), image_spec(GROUP), image_spec(SENT), row_spec(width), row_spec(width)]
        + [whole(a.shape) for a in weights],
        [
            shaped((total, GROUP, cols, width), BF16),
            shaped((total * TOKENS, width), F32),
            shaped((total * TOKENS, width), BF16),
            shaped((total, SENT, cols, width), BF16),
        ]
        + accumulated,
        [image_spec(GROUP), row_spec(width), row_spec(width), image_spec(SENT)]
        + [whole(a.shape) for a in accumulated],
        scratch=[
            pltpu.VMEM((per_step, GROUP, PAD_COLS, width), BF16),
            pltpu.VMEM((per_step, GROUP, PAD_COLS, width), BF16),
            pltpu.VMEM((2, width, hidden), F32),
        ],
        flops=total * TOKENS * width * width * 54,
        vmem=60,
    )


def pick_heads(stacked):
    parts = stacked.reshape(PER_BLOCK, TOKENS, LANES)
    lane = lax.broadcasted_iota(jnp.int32, (TOKENS, LANES), 1)
    picked = parts[PER_BLOCK - 1]
    for head in range(PER_BLOCK - 2, -1, -1):
        picked = jnp.where(lane < (head + 1) * HEAD_DIM, parts[head], picked)
    return picked


def back_kernel(count, first_call, last_call, where, normed, qkv, probs_ref, grad_att, mask, a_proj, *refs):
    carried = () if first_call else refs[:3]
    (grads, o_small, o_pair, o_first, o_second, a_w, packed) = refs[len(carried) :]
    width = normed.shape[1]
    step = pl.program_id(0)

    @pl.when(step == 0)
    def _():
        for index, ref in enumerate((o_small, o_pair, a_w)):
            ref[...] = jnp.zeros_like(ref) if first_call else carried[index][...]

    masks = mask[...]
    for image in range(count):
        rows = slice(image * TOKENS, (image + 1) * TOKENS)
        for block in range(HEADS // PER_BLOCK):
            at = block * LANES
            here = slice(block * STACK, (block + 1) * STACK)
            query = qkv[rows, at : at + LANES]
            keys = stack_heads(qkv[rows, width + at : width + at + LANES], masks)
            vals = stack_heads(qkv[rows, 2 * width + at : 2 * width + at + LANES], masks)
            grad = grad_att[rows, at : at + LANES]
            probs = probs_ref[image, here, :]
            exact = probs.astype(F32).reshape(PER_BLOCK, TOKENS, TOKENS)
            grad_probs = dot_nt(vals, grad).reshape(PER_BLOCK, TOKENS, TOKENS)
            inner = jnp.sum(grad_probs * exact, axis=1, keepdims=True)
            grad_scores = (exact * (grad_probs - inner)).reshape(STACK, TOKENS).astype(BF16)
            o_pair[here, :] += grad_scores.astype(F32)
            grads[rows, at : at + LANES] = (dot_tn(grad_scores, keys) * SCALE).astype(BF16)
            grads[rows, width + at : width + at + LANES] = (
                pick_heads(dot(grad_scores, query)) * SCALE
            ).astype(BF16)
            grads[rows, 2 * width + at : 2 * width + at + LANES] = pick_heads(
                dot(probs, grad)
            ).astype(BF16)
    all_grads = grads[...]
    a_w[...] += dot(normed[...].T, all_grads)
    o_small[0:1, :] += column_sum(all_grads[:, :width].astype(F32))
    o_small[1:2, :] += column_sum(all_grads[:, 2 * width :].astype(F32))

    @pl.when(step == pl.num_programs(0) - 1)
    def _():
        if last_call:
            core = where[1]
            for part in range(3):
                packed[part] = a_w[:, part * width : (part + 1) * width].astype(BF16)
            packed[3] = a_proj[...].astype(BF16)
            for part in range(2):
                o_first[part] = packed[2 * core + part]
                o_second[part] = packed[2 - 2 * core + part]
        else:
            o_first[...] = a_w[...]
            o_second[...] = jnp.zeros_like(o_second)


def attend_back(where, first, count, per_step, saved, mask, grad_proj, carried, so_far, last_call, after):
    normed, qkv, probs, grad_att = saved
    width = normed.shape[1]
    begin = first // per_step
    rows = per_step * TOKENS
    extra = () if carried is None else tuple(carried)
    row_spec = lambda w: pl.BlockSpec((rows, w), lambda i: (i + begin, 0))
    fixed = (mask, grad_proj)
    if last_call:
        first_shape = second_shape = shaped((2, width, width), BF16)
    else:
        first_shape = shaped((width, 3 * width), F32)
        second_shape = shaped((8, LANES), F32)
    accumulated = [
        shaped((8, width), F32),
        shaped((HEADS * TOKENS, TOKENS), F32),
        first_shape,
        second_shape,
    ]
    return launch(
        partial(back_kernel, per_step, carried is None, last_call),
        "attend_back",
        (count // per_step,),
        (where, normed, qkv, probs, grad_att, *fixed, *extra),
        [
            pl.BlockSpec(memory_space=pltpu.SMEM),
            row_spec(width),
            row_spec(3 * width),
            pl.BlockSpec((per_step, HEADS * TOKENS, TOKENS), lambda i: (i + begin, 0, 0)),
            row_spec(width),
        ]
        + [whole(a.shape) for a in (*fixed, *extra)],
        [shaped(qkv.shape, BF16)] + accumulated,
        [row_spec(3 * width)] + [whole(a.shape) for a in accumulated],
        so_far=so_far,
        scratch=[
            pltpu.VMEM((width, 3 * width), F32),
            pltpu.VMEM((4, width, width), BF16),
        ],
        flops=count * TOKENS * width * width * 18,
        after=after,
        vmem=60,
    )


def images_kernel(first_call, where, grads, x_ref, grad_mid, gain, weight, *refs):
    carried = () if first_call else refs[:1]
    (gi_kept, gi_send, o_small, placed) = refs[len(carried) :]

    @pl.when(pl.program_id(0) == 0)
    def _():
        o_small[...] = jnp.zeros_like(o_small) if first_call else carried[0][...]

    grad_normed = dot_nt(grads[...], weight[...]).astype(BF16).astype(F32)
    hat, inverse = normalise(x_ref[...].astype(F32))
    o_small[0:1, :] += column_sum(grad_normed * hat)
    o_small[1:2, :] += column_sum(grad_normed)
    grad_image = grad_mid[...] + normalise_back(grad_normed * gain[...][None, :], hat, inverse)
    placed[...] = grad_image.reshape(placed.shape)
    return_rows(where[0], placed, gi_kept, gi_send)


def image_grads(where, first, count, per_step, grads, x, grad_mid, gain, weight, shape, carried, so_far, after):
    total, _, cols, width = shape
    begin = first // per_step
    rows = per_step * TOKENS
    row_spec = lambda w: pl.BlockSpec((rows, w), lambda i: (i + begin, 0))
    fixed = (gain, weight, *carried)
    return launch(
        partial(images_kernel, not carried),
        "image_grads",
        (count // per_step,),
        (where, grads, x, grad_mid, *fixed),
        [pl.BlockSpec(memory_space=pltpu.SMEM), row_spec(3 * width), row_spec(width), row_spec(width)]
        + [whole(a.shape) for a in fixed],
        [
            shaped((total, GROUP, cols, width), F32),
            shaped((count, SENT, cols, width), BF16),
            shaped((8, width), F32),
        ],
        [
            pl.BlockSpec((per_step, GROUP, cols, width), lambda i: (i + begin, 0, 0, 0)),
            pl.BlockSpec((per_step, SENT, cols, width), lambda i: (i, 0, 0, 0)),
            whole((8, width)),
        ],
        so_far=so_far,
        scratch=[pltpu.VMEM((per_step, GROUP, PAD_COLS, width), F32)],
        flops=count * TOKENS * width * width * 6,
        after=after,
        vmem=32,
    )


def swap(value, flip):
    bands, batches = lax.axis_size("band"), lax.axis_size("batch")
    pairs = []
    for band in range(bands):
        for batch in range(batches):
            other = (band ^ flip[0]) * batches + (batch ^ flip[1])
            pairs.append((band * batches + batch, other))
    return lax.ppermute(value, ("band", "batch"), pairs)


def in_plane(value, d):
    return swap(value, (d >> 1, (d & 1) << 1))


PLANE = 4
ALONG = 4


def tree_sum(values):
    while len(values) > 1:
        values = [values[i] + values[i + 1] for i in range(0, len(values), 2)]
    return values[0]


def split_kernel(slot, count, small_rows, where, *refs):
    *refs, token = refs
    token[...] = jnp.zeros_like(token)
    outs = refs[-count - (1 if small_rows else 0) :]
    ins = refs[: len(refs) - len(outs)]
    me = where[slot]
    rows = outs[0].shape[0]
    if small_rows:
        ins, small_ins = ins[:small_rows], ins[small_rows:]
        small = tree_sum([r[...] if r.dtype == F32 else get_pair(r, r.shape[0] - 2 * SMALL) for r in small_ins])

    def total(index):
        start = pl.multiple_of(index * rows, rows)
        return tree_sum([ref[pl.ds(start, rows), :].astype(F32) for ref in ins])

    for d in range(count):
        outs[d][0:rows, :] = total(me ^ d).astype(outs[d].dtype)
        if small_rows and d > 0:
            put_pair(outs[d], rows, small)
    if small_rows:
        high = small.astype(BF16).astype(F32)
        outs[count][...] = high + (small - high).astype(BF16).astype(F32)


def split_share(where, slot, count, values, after, flops=0):
    rows, width = values[0].shape
    size = rows // count
    outs = [shaped((size, width), F32 if d == 0 else BF16) for d in range(count)] + [TOKEN]
    return small_launch(
        partial(split_kernel, slot, count, 0), "split_share", (where, *values), outs, after=after,
        flops=flops,
    )


def split_with_small(where, slot, count, values, smalls, after):
    rows, width = values[0].shape
    size = rows // count
    outs = [shaped((size, width), F32)] + [shaped((size + 2 * SMALL, width), BF16)] * (count - 1)
    outs += [shaped((SMALL, width), F32), TOKEN]
    return small_launch(
        partial(split_kernel, slot, count, len(values)), "split_with_small", (where, *values, *smalls), outs, after=after,
    )


def join_kernel(count, *refs):
    early, late = refs[:count], refs[count : 2 * count]
    small, share, small_out = refs[2 * count :]
    rows, more = early[0].shape[0], late[0].shape[0]
    share[0:rows, :] = tree_sum([r[...].astype(F32) for r in early]).astype(BF16)
    share[rows : rows + more, :] = tree_sum([r[0:more, :].astype(F32) for r in late]).astype(BF16)
    small_out[...] = tree_sum([small[...]] + [get_pair(r, more) for r in late[1:]])


def join_shares(early, late, small, after):
    rows, width = early[0].shape
    return small_launch(
        partial(join_kernel, len(early)),
        "join_shares",
        (*early, *late, small),
        [shaped((rows + late[0].shape[0], width), BF16), shaped((SMALL, width), F32)],
        after=after,
    )


def lay_kernel(slot, where, *refs):
    parts, (small, other, out) = refs[:-3], refs[-3:]
    rows = parts[0].shape[0]
    for d, ref in enumerate(parts):
        out[pl.ds(pl.multiple_of((where[slot] ^ d) * rows, rows), rows), :] = ref[...]
    put_pair(out, len(parts) * rows, small[...] + other[...])


def along(value, d):
    return swap(value, (0, 4 * d))


def spread(pieces, send):
    return [pieces[0]] + [send(piece, d) for d, piece in enumerate(pieces) if d > 0]


def gather_along(where, share, small, after):
    rows, width = share.shape
    parts = spread([share] * ALONG, along)
    return small_launch(
        partial(lay_kernel, 3),
        "lay",
        (where, *parts, small, swap(small, (0, 1))),
        [shaped((ALONG * rows + 2 * SMALL, width), BF16)],
        after=after,
    )[0]


def halve_kernel(across, along_row, low, high):
    low[...] = across[0 : low.shape[0], :]
    high[...] = along_row[low.shape[0] :, :]


def collect_kernel(own, across, along_row, low, high, out, small):
    rows, cut = out.shape[1], low.shape[0]
    out[0] = along_row[0:rows, :]
    out[1] = across[0:rows, :]
    out[2, 0:cut, :] = low[...]
    out[2, cut:rows, :] = high[0 : rows - cut, :]
    far = get_pair(high, rows - cut)
    small[...] = (get_pair(own, rows) + get_pair(along_row, rows)) + (get_pair(across, rows) + far)


def gather_plane(quarter, after):
    theirs = swap(quarter, (0, 1))
    rows, width = quarter.shape
    across, along_row = in_plane(quarter, 2), in_plane(quarter, 1)
    cut = rows // 32 * 16
    low, high = small_launch(
        halve_kernel, "halve", (across, along_row), [shaped((cut, width), BF16), shaped((rows - cut, width), BF16)],
        after=after,
    )
    mine, small = small_launch(
        collect_kernel,
        "collect",
        (quarter, across, along_row, in_plane(low, 1), in_plane(high, 2)),
        [shaped((PLANE - 1, rows - 2 * SMALL, width), BF16), shaped((SMALL, width), F32)],
    )
    return small, (quarter, mine), (theirs, swap(mine, (0, 1)))


def unpack_kernel(flip, early, where, first, rest, o_w1, o_w2, o_qkv, o_proj, feed_buf, att_buf, sems):
    me, side = where[2], where[1] ^ flip
    width = o_proj.shape[0]
    late = width // 2 // ALONG
    low, high = slice(0, width // 2), slice(width // 2, width)
    for d in range(PLANE):
        quarter = first if d == 0 else rest.at[d - 1]
        for share in range(ALONG):
            start = share * (early + late)
            feed_buf[d, share * early : (share + 1) * early, :] = quarter[start : start + early, :].astype(F32)
            att_buf[me ^ d, share * late : (share + 1) * late, :] = quarter[
                start + early : start + early + late, :
            ].astype(F32)

    def send(copies):
        for index, (source, target) in enumerate(copies):
            pltpu.make_async_copy(source, target, sems.at[index]).start()
        for index, (source, target) in enumerate(copies):
            pltpu.make_async_copy(source, target, sems.at[index]).wait()

    def place(d):
        return pl.ds(pl.multiple_of((me ^ d) * width, width), width)

    def halves(target, cols, at):
        return [(att_buf.at[at], target.at[low, cols]), (att_buf.at[at + 1], target.at[high, cols])]

    @pl.when(side == 0)
    def _():
        copies = [(feed_buf.at[d], o_w1.at[:, place(d)]) for d in range(PLANE)]
        copies += halves(o_qkv, slice(0, width), 0) + halves(o_qkv, slice(width, 2 * width), 2)
        send(copies)

    @pl.when(side == 1)
    def _():
        for d in range(PLANE):
            feed_buf[d] = feed_buf[d].T
        copies = [(feed_buf.at[d], o_w2.at[place(d), :]) for d in range(PLANE)]
        copies += halves(o_qkv, slice(2 * width, 3 * width), 0) + halves(o_proj, slice(0, width), 2)
        send(copies)


def unpack(flip, early, where, half, shapes, so_far):
    width = half[0].shape[1]
    vector = pl.BlockSpec(memory_space=pltpu.VMEM)
    return launch(
        partial(unpack_kernel, flip, early),
        "unpack",
        (),
        (where, *half),
        [pl.BlockSpec(memory_space=pltpu.SMEM), vector, vector],
        [shaped(shape, F32) for shape in shapes],
        [pl.BlockSpec(memory_space=pl.ANY)] * len(shapes),
        so_far=so_far,
        scratch=[
            pltpu.VMEM((PLANE, width, width), F32),
            pltpu.VMEM((PLANE, width // 2, width), F32),
            pltpu.SemaphoreType.DMA((2 * PLANE,)),
        ],
        vmem=24,
    )


def body(images, cotangent, norm1_gain, norm1_shift, qkv_weight, qv_bias, proj_weight, proj_bias, *rest):
    pos = rest[:13]
    norm2_gain, norm2_shift, fc1_weight, fc1_bias, fc2_weight, fc2_bias = rest[13:]
    total, _, cols, width = images.shape
    hidden = fc1_weight.shape[1]
    per_step = 4
    band, batch = lax.axis_index("band"), lax.axis_index("batch")
    where = jnp.stack([band, batch % 2, band * 2 + batch // 2 % 2, batch // 4 % ALONG]).astype(jnp.int32)
    head_of_row = np.arange(STACK)[:, None] // TOKENS
    mask = jnp.asarray(head_of_row == np.arange(LANES)[None, :] // HEAD_DIM, BF16)
    to_partner = lambda value: swap(value, (1, 0))
    pos = (*pos[:12], pos[12].T)

    later = (total // per_step * 2 // 5) * per_step
    image_chunks = [(0, later), (later, total - later)]
    packed, token = pack_rows((images,), [(0, *image_chunks[0])])
    received = to_partner(packed)
    later_packed, cot_packed, _ = pack_rows(
        (images, cotangent), [(0, *image_chunks[1]), (1, 0, total)], (token,)
    )
    pair, later_packed, cot_packed = pair_bias(pos, (later_packed, cot_packed))
    later_received = to_partner(later_packed)
    norm_one = (norm1_gain, norm1_shift, qkv_weight, qv_bias, pair, mask)
    so_far = attend(where, images, received, 0, per_step, *norm_one, (), ())
    _, cot_packed = small_launch(
        token_kernel, "order", (), [TOKEN], after=(*so_far[:1], later_received), vmem=60, through=(cot_packed,)
    )
    cot_rows = to_partner(cot_packed)
    so_far = attend(where, images, later_received, later, per_step, *norm_one, so_far, ())
    x, normed, qkv, probs, att = so_far
    weights = (proj_weight, proj_bias, norm2_gain, norm2_shift, fc1_weight, fc1_bias, fc2_weight, fc2_bias)
    result = feed(where, cotangent, cot_rows, per_step, x, att, weights)
    out_images, grad_mid, grad_att, out_sent, feed_small, feed_b1, mine, theirs, grad_proj = result
    out_rows = to_partner(out_sent)
    flat = lambda value: value.reshape(-1, width)
    early = [flat(mine), swap(flat(theirs), (0, 1))]

    saved = (normed, qkv, probs, grad_att)
    chunks = [(0, total - later), (total - later, later)]
    result = attend_back(where, *chunks[0], per_step, saved, mask, grad_proj, None, (), False, ())
    *pieces, token = split_share(where, 2, PLANE, early, (result[1],))
    early = spread(pieces, in_plane)
    result = attend_back(where, *chunks[1], per_step, saved, mask, grad_proj, result[1:4], result[:1], True,
                         (token, out_rows))
    grads, att_small, grad_pair = result[:3]
    mine, theirs = flat(result[3]), flat(result[4])
    *pieces, token = split_share(where, 3, ALONG, early, (att_small,), 5e9)
    early = spread(pieces, along)
    *pieces, token = split_share(where, 2, PLANE, [mine, swap(theirs, (0, 1))], (token,))
    late = spread(pieces, in_plane)
    grad_images, sent, norm_small = image_grads(where, 0, total, per_step, grads, x, grad_mid, norm1_gain,
                                                qkv_weight, images.shape, (), (), (token,))
    grad_rows = to_partner(sent)
    small = gather_small(feed_small, feed_b1, att_small, norm_small, grad_pair)
    *pieces, small, _ = split_with_small(where, 3, ALONG, late, [small], early[1:])
    late = spread(pieces, along)
    share, small = join_shares(early, late, small, ())
    stride = PLANE * ALONG
    while stride < lax.axis_size("batch"):
        share = (share.astype(F32) + swap(share, (0, stride)).astype(F32)).astype(BF16)
        small = small + swap(small, (0, stride))
        stride *= 2
    out_images, token = merge_rows(out_rows, out_images, 0)
    quarter = gather_along(where, share, small, (token,))
    grad_images, token = merge_rows(grad_rows, grad_images, 0)
    small, half, other_half = gather_plane(quarter, (token,))
    smalls = finish_small(pos, small, hidden)
    shapes = [w.shape for w in (fc1_weight, fc2_weight, qkv_weight, proj_weight)]
    large = unpack(0, early[0].shape[0], where, half, shapes, ())
    grad_fc1, grad_fc2, grad_qkv, grad_proj = unpack(1, early[0].shape[0], where, other_half, shapes, large)
    n1_gain, n1_shift, qv, proj_b, n2_gain, n2_shift, fc1_b, fc2_b = smalls[:8]
    return (out_images, grad_images, n1_gain, n1_shift, grad_qkv, qv, grad_proj, proj_b, *smalls[8:20], smalls[20].T,
            n2_gain, n2_shift, grad_fc1, fc1_b, grad_fc2, fc2_b)


def solution(mesh):
    tokens = P("batch", "band", None, None)
    return jax.shard_map(
        body,
        mesh=mesh,
        in_specs=(tokens, tokens) + (P(),) * 25,
        out_specs=(tokens, tokens) + (P(),) * 25,
        check_vma=False,
    )
```

```python
import math
from functools import partial

import jax
import jax.numpy as jnp
import numpy as np
from jax import lax
from jax.experimental import pallas as pl
from jax.experimental.pallas import tpu as pltpu
from jax.sharding import PartitionSpec as P

HEADS = 12
GROUP = 7
HEAD_DIM = 32
SPAN = 2 * GROUP - 1
HIGH = lax.Precision.HIGHEST
EPSILON = 1e-05
SCALE = HEAD_DIM**-0.5
MASKED = -1e30
PAD_COLS = 16
TOKENS = GROUP * PAD_COLS
LANES = 128
PER_BLOCK = LANES // HEAD_DIM
STACK = PER_BLOCK * TOKENS
KEPT = (GROUP + 1) // 2
SENT = GROUP - KEPT
OFFSETS = 176
WIDE = SPAN * PAD_COLS
F32 = jnp.float32
BF16 = jnp.bfloat16


def dot(a, b, precision=None):
    return lax.dot_general(a, b, (((1,), (0,)), ((), ())), precision=precision, preferred_element_type=F32)


def dot_nt(a, b, precision=None):
    return lax.dot_general(a, b, (((1,), (1,)), ((), ())), precision=precision, preferred_element_type=F32)


def dot_tn(a, b, precision=None):
    return lax.dot_general(a, b, (((0,), (0,)), ((), ())), precision=precision, preferred_element_type=F32)


def whole(shape):
    zeros = (0,) * len(shape)
    return pl.BlockSpec(shape, lambda *_: zeros, pipeline_mode=pl.Buffered(1))


def normalise(values):
    mean = jnp.mean(values, axis=-1, keepdims=True)
    centred = values - mean
    inverse = lax.rsqrt(jnp.mean(centred * centred, axis=-1, keepdims=True) + EPSILON)
    return centred * inverse, inverse


def normalise_back(grad_hat, hat, inverse):
    first = jnp.mean(grad_hat, axis=-1, keepdims=True)
    second = jnp.mean(grad_hat * hat, axis=-1, keepdims=True)
    return inverse * (grad_hat - first - hat * second)


def gelu_both(v):
    cdf = 0.5 + 0.5 * lax.erf(v * (0.5**0.5))
    density = jnp.exp(-0.5 * v * v) * ((2.0 * np.pi) ** -0.5)
    return v * cdf, cdf + v * density


def column_sum(values):
    return jnp.sum(values, axis=0, keepdims=True)


SMALL = 24


def launch(kernel, name, grid, inputs, in_specs, out_shape, out_specs, so_far=(), scratch=(), flops=0,
           after=(), vmem=16, through=()):
    count, held = len(inputs), len(so_far) + len(after) + len(through)
    own = len(out_shape)
    hand = {count + len(so_far) + len(after) + i: own + i for i in range(len(through))}
    inner = kernel
    if held:
        kernel = lambda *refs: inner(
            *refs[:count], *refs[count + held : count + held + own], *refs[count + held + own + len(through) :]
        )
    moved = sum(a.size * a.dtype.itemsize for a in (*inputs, *out_shape))
    return pl.pallas_call(
        kernel,
        grid=grid,
        in_specs=list(in_specs) + [pl.BlockSpec(memory_space=pl.ANY)] * held,
        out_specs=list(out_specs) + [pl.BlockSpec(memory_space=pl.ANY)] * len(through),
        out_shape=list(out_shape) + [shaped(a.shape, a.dtype) for a in through],
        input_output_aliases={count + i: i for i in range(len(so_far))} | hand,
        scratch_shapes=list(scratch),
        compiler_params=pltpu.CompilerParams(vmem_limit_bytes=vmem * 2**20),
        cost_estimate=pl.CostEstimate(flops=int(flops), bytes_accessed=int(moved), transcendentals=0),
        name=name,
    )(*inputs, *so_far, *after, *through)


def small_launch(kernel, name, inputs, out_shape, scratch=(), flops=0, after=(), vmem=16, through=()):
    specs = [pl.BlockSpec(memory_space=pltpu.SMEM if a.dtype == jnp.int32 else pltpu.VMEM) for a in inputs]
    outs = [pl.BlockSpec(memory_space=pltpu.VMEM)] * len(out_shape)
    return launch(kernel, name, (), inputs, specs, out_shape, outs, scratch=scratch, flops=flops, after=after, vmem=vmem,
                  through=through)


def shaped(shape, dtype):
    return jax.ShapeDtypeStruct(shape, dtype)


FEED_PART = 512
TOKEN = shaped((8, LANES), F32)


def token_kernel(token):
    token[...] = jnp.zeros_like(token)


def merge_kernel(source, target, token):
    target[...] = source[...].astype(target.dtype)
    token[...] = jnp.zeros_like(token)


def pack_kernel(pieces, *refs):
    count = 1 + max(piece[0] for piece in pieces)
    sources, outs, (token, sems) = refs[:count], refs[count:-2], refs[-2:]
    token[...] = jnp.zeros_like(token)
    copies = []
    for (source, first, images), out in zip(pieces, outs):
        for row in range(SENT):
            copies.append(
                pltpu.make_async_copy(
                    sources[source].at[first : first + images, 2 * row + 1], out.at[:, row], sems.at[len(copies)]
                )
            )
    for copy in copies:
        copy.start()
    for copy in copies:
        copy.wait()


def pack_rows(sources, pieces, after=()):
    _, _, cols, width = sources[0].shape
    vector = pl.BlockSpec(memory_space=pltpu.VMEM)
    return launch(
        partial(pack_kernel, pieces),
        "pack_rows",
        (),
        sources,
        [pl.BlockSpec(memory_space=pl.ANY)] * len(sources),
        [shaped((count, SENT, cols, width), BF16) for _, _, count in pieces] + [TOKEN],
        [vector] * (len(pieces) + 1),
        scratch=[pltpu.SemaphoreType.DMA((SENT * len(pieces),))],
        after=after,
        vmem=60,
    )


def merge_rows(received, target, first):
    count, _, cols, width = received.shape
    unit = math.gcd(first, count)
    begin = first // unit
    return launch(
        merge_kernel,
        "merge_rows",
        (count // unit, SENT),
        (received,),
        [pl.BlockSpec((unit, 1, cols, width), lambda i, r: (i, r, 0, 0))],
        [shaped(target.shape, target.dtype), TOKEN],
        [pl.BlockSpec((unit, 1, cols, width), lambda i, r: (i + begin, 2 * r + 1, 0, 0)), whole(TOKEN.shape)],
        so_far=(target,),
    )


def position_layers(refs):
    (in_w, in_b, g1, s1, w1, b1, g2, s2, w2, b2, g3, s3, _) = refs
    width = in_w.shape[1]
    offset = lax.broadcasted_iota(jnp.int32, (OFFSETS, width), 0)
    rows = (offset // SPAN - (GROUP - 1)).astype(F32)
    cols = (offset % SPAN - (GROUP - 1)).astype(F32)
    hidden = rows * in_w[0:1, :] + cols * in_w[1:2, :] + in_b[...][None, :]
    kept = []
    for gain, shift, weight, bias in ((g1, s1, w1, b1), (g2, s2, w2, b2), (g3, s3, None, None)):
        hat, inverse = normalise(hidden)
        active, slope = gelu_both(hat * gain[...][None, :] + shift[...][None, :])
        kept.append((hat, inverse, active, slope))
        if weight is not None:
            hidden = dot(active, weight[...], HIGH) + bias[...][None, :]
    return rows, cols, kept


def pick_offsets(place):
    offset = lax.broadcasted_iota(jnp.int32, (OFFSETS, WIDE), 0)
    lane = lax.broadcasted_iota(jnp.int32, (OFFSETS, WIDE), 1)
    wanted = lane // PAD_COLS * SPAN + lane % PAD_COLS // 2 - place + GROUP - 1
    return jnp.where(offset == wanted, 1.0, 0.0).astype(F32)


def bias_kernel(*refs):
    ins, (out, strip) = refs[:13], refs[13:]
    _, _, kept = position_layers(ins)
    table = dot_nt(ins[12][...], kept[2][2], HIGH)
    lane = lax.broadcasted_iota(jnp.int32, (HEADS, WIDE), 1)
    even = lane % 2 == 0
    strip[...] = jnp.full(strip.shape, MASKED, F32)
    for place in range(GROUP):
        spread = dot(table, pick_offsets(place), HIGH)
        strip[:, 2 * place, 0:WIDE] = jnp.where(even, spread, MASKED)
        strip[:, 2 * place + 1, 0:WIDE] = jnp.where(even, MASKED, spread)
    out[...] = jnp.zeros_like(out)
    for row in range(GROUP):
        start = (GROUP - 1 - row) * PAD_COLS
        out[:, row * PAD_COLS : (row + 1) * PAD_COLS, 0:TOKENS] = strip[:, :, start : start + TOKENS]


def pair_bias(pos, through):
    return small_launch(
        bias_kernel,
        "pair_bias",
        pos,
        [shaped((HEADS, TOKENS, LANES), F32)],
        [pltpu.VMEM((HEADS, PAD_COLS, 2 * LANES), F32)],
        through=through,
        vmem=60,
    )


def put_pair(ref, start, values):
    high = values.astype(BF16)
    ref[start : start + SMALL, :] = high
    ref[start + SMALL : start + 2 * SMALL, :] = (values - high.astype(F32)).astype(BF16)


def get_pair(ref, start):
    return ref[start : start + SMALL, :].astype(F32) + ref[start + SMALL : start + 2 * SMALL, :].astype(F32)


def gather_small_kernel(feed_small, feed_b1, att_small, norm_small, grad_pair, out, small):
    width = feed_small.shape[1]
    strip = jnp.zeros((HEADS, PAD_COLS, WIDE), F32)
    for row in range(GROUP):
        start = (GROUP - 1 - row) * PAD_COLS
        piece = grad_pair[:, row * PAD_COLS : (row + 1) * PAD_COLS, 0:TOKENS]
        strip = strip + jnp.pad(piece, ((0, 0), (0, 0), (start, WIDE - start - TOKENS)))
    table = jnp.zeros((HEADS, OFFSETS), F32)
    for place in range(GROUP):
        folded = strip[:, 2 * place, :] + strip[:, 2 * place + 1, :]
        table = table + dot_nt(folded, pick_offsets(place), HIGH)
    small[...] = jnp.zeros_like(small)
    small[0:4, :] = feed_small[0:4, :]
    small[4:6, :] = norm_small[0:2, :]
    small[6:8, :] = att_small[0:2, :]
    for part in range(feed_b1.shape[1] // width):
        small[8 + part : 9 + part, :] = feed_b1[:, part * width : (part + 1) * width]
    small[12 : 12 + HEADS, 0:OFFSETS] = table
    put_pair(out, 0, small[...])


def gather_small(feed_small, feed_b1, att_small, norm_small, grad_pair):
    width = feed_small.shape[1]
    return small_launch(
        gather_small_kernel,
        "gather_small",
        (feed_small, feed_b1, att_small, norm_small, grad_pair.reshape(HEADS, TOKENS, LANES)),
        [shaped((2 * SMALL, width), BF16)],
        [pltpu.VMEM((SMALL, width), F32)],
    )[0]


def finish_small_kernel(*refs):
    ins, small, outs = refs[:13], refs[13], refs[14:]
    (in_w, in_b, g1, s1, w1, b1, g2, s2, w2, b2, g3, s3, w3) = ins
    (o_n1_gain, o_n1_shift, o_qv, o_proj_b, o_n2_gain, o_n2_shift, o_fc1_b, o_fc2_b) = outs[:8]
    (o_in_w, o_in_b, o_g1, o_s1, o_w1, o_b1, o_g2, o_s2, o_w2, o_b2, o_g3, o_s3, o_w3) = outs[8:]
    o_n2_gain[...] = small[0, :]
    o_n2_shift[...] = small[1, :]
    o_fc2_b[...] = small[2, :]
    o_proj_b[...] = small[3, :]
    o_n1_gain[...] = small[4, :]
    o_n1_shift[...] = small[5, :]
    o_qv[...] = small[6:8, :]
    width = small.shape[1]
    for part in range(o_fc1_b.shape[0] // width):
        o_fc1_b[part * width : (part + 1) * width] = small[8 + part, :]
    rows, cols, kept = position_layers(ins)
    table = small[12 : 12 + HEADS, 0:OFFSETS]
    o_w3[...] = dot(table, kept[2][2], HIGH)
    grad_active = dot(table.T, w3[...], HIGH)
    stages = (
        (g3, o_g3, o_s3, o_b2, o_w2, w2),
        (g2, o_g2, o_s2, o_b1, o_w1, w1),
        (g1, o_g1, o_s1, o_in_b, None, None),
    )
    for level, (gain, o_gain, o_shift, o_bias, o_weight, weight) in zip((2, 1, 0), stages):
        hat, inverse, _, slope = kept[level]
        grad_norm = grad_active * slope
        o_gain[...] = jnp.sum(grad_norm * hat, axis=0)
        o_shift[...] = jnp.sum(grad_norm, axis=0)
        grad_hidden = normalise_back(grad_norm * gain[...][None, :], hat, inverse)
        o_bias[...] = jnp.sum(grad_hidden, axis=0)
        if weight is not None:
            o_weight[...] = dot(kept[level - 1][2].T, grad_hidden, HIGH)
            grad_active = dot_nt(grad_hidden, weight[...], HIGH)
        else:
            o_in_w[0:1, :] = column_sum(grad_hidden * rows)
            o_in_w[1:2, :] = column_sum(grad_hidden * cols)


def finish_small(pos, small, hidden):
    width = small.shape[1]
    shapes = [(width,), (width,), (2, width), (width,), (width,), (width,), (hidden,), (width,)]
    return small_launch(
        finish_small_kernel,
        "finish_small",
        (*pos, small),
        [shaped(s, F32) for s in shapes] + [shaped(p.shape, F32) for p in pos],
    )


def stack_heads(block, mask):
    return jnp.concatenate([block] * PER_BLOCK, axis=0) * mask


def two_images(two):
    return [slice(image * TOKENS, (image + 1) * TOKENS) for image in (2 * two, 2 * two + 1)]


def on_diagonal(blocks):
    rest = jnp.zeros((LANES - TOKENS, LANES), BF16)
    zero = jnp.zeros((LANES, LANES), BF16)
    first, second = [jnp.concatenate([block, rest], axis=0) for block in blocks]
    return jnp.concatenate(
        [jnp.concatenate([first, zero], axis=1), jnp.concatenate([zero, second], axis=1)], axis=0
    )


def side_by_side(blocks, mask):
    return jnp.concatenate([stack_heads(block, mask) for block in blocks], axis=1)


def place_rows(band, kept_ref, received_ref, padded):
    upper = band * SENT
    lower = (1 - band) * KEPT
    for row in range(KEPT):
        padded[:, row + upper, 0 : 2 * GROUP, :] = kept_ref[:, 2 * row]
    for row in range(SENT):
        padded[:, row + lower, 0 : 2 * GROUP, :] = received_ref[:, row]


def return_rows(band, placed, kept_ref, sent_ref):
    upper = band * SENT
    lower = (1 - band) * KEPT
    for row in range(KEPT):
        kept_ref[:, 2 * row] = placed[:, row + upper, 0 : 2 * GROUP, :]
    for row in range(SENT):
        sent_ref[:, row] = placed[:, row + lower, 0 : 2 * GROUP, :].astype(sent_ref.dtype)


def attend_kernel(count, where, images, received, gain, shift, weight, bias, pair, mask,
                  x_out, normed_out, qkv_out, probs_out, att_out, padded):
    width = images.shape[3]

    @pl.when(pl.program_id(0) == 0)
    def _():
        padded[...] = jnp.zeros_like(padded)

    place_rows(where[0], images, received, padded)
    x = padded[...].reshape(count * TOKENS, width)
    x_out[...] = x
    hat, _ = normalise(x.astype(F32))
    normed = (hat * gain[...][None, :] + shift[...][None, :]).astype(BF16)
    normed_out[...] = normed
    piece = dot(normed, weight[...])
    qkv_out[:, 0:width] = (piece[:, 0:width] + bias[0:1, :]).astype(BF16)
    qkv_out[:, width : 2 * width] = piece[:, width : 2 * width].astype(BF16)
    qkv_out[:, 2 * width :] = (piece[:, 2 * width :] + bias[1:2, :]).astype(BF16)
    masks = mask[...]
    for two in range(count // 2):
        both = two_images(two)
        for block in range(HEADS // PER_BLOCK):
            at = block * LANES
            here = slice(block * STACK, (block + 1) * STACK)
            query = on_diagonal([qkv_out[rows, at : at + LANES] for rows in both])
            keys = side_by_side([qkv_out[rows, width + at : width + at + LANES] for rows in both], masks)
            scores = dot_nt(keys, query) * SCALE + jnp.concatenate([pair[here, :]] * 2, axis=1)
            scores = scores.reshape(PER_BLOCK, TOKENS, 2 * LANES)
            probs = jnp.exp(scores - jnp.max(scores, axis=1, keepdims=True))
            probs = probs * (1.0 / jnp.sum(probs, axis=1, keepdims=True))
            probs = probs.astype(BF16).reshape(STACK, 2 * LANES)
            probs_out[two, here, :] = probs
            for half, rows in enumerate(both):
                vals = stack_heads(qkv_out[rows, 2 * width + at : 2 * width + at + LANES], masks)
                attended = dot_tn(probs[:, half * LANES : (half + 1) * LANES], vals)
                att_out[rows, at : at + LANES] = attended[0:TOKENS, :].astype(BF16)


def attend(where, images, received, first, per_step, gain, shift, weight, bias, pair, mask, so_far, through):
    total, _, cols, width = images.shape
    count = received.shape[0]
    begin = first // per_step
    rows = per_step * TOKENS
    row_spec = lambda w: pl.BlockSpec((rows, w), lambda i: (i + begin, 0))
    fixed = (gain, shift, weight, bias, pair.reshape(HEADS * TOKENS, LANES), mask)
    return launch(
        partial(attend_kernel, per_step),
        "attend",
        (count // per_step,),
        (where, images, received, *fixed),
        [
            pl.BlockSpec(memory_space=pltpu.SMEM),
            pl.BlockSpec((per_step, GROUP, cols, width), lambda i: (i + begin, 0, 0, 0)),
            pl.BlockSpec((per_step, SENT, cols, width), lambda i: (i, 0, 0, 0)),
        ]
        + [whole(a.shape) for a in fixed],
        [
            shaped((total * TOKENS, width), BF16),
            shaped((total * TOKENS, width), BF16),
            shaped((total * TOKENS, 3 * width), BF16),
            shaped((total // 2, HEADS * TOKENS, 2 * LANES), BF16),
            shaped((total * TOKENS, width), BF16),
        ],
        [
            row_spec(width),
            row_spec(width),
            row_spec(3 * width),
            pl.BlockSpec((per_step // 2, HEADS * TOKENS, 2 * LANES), lambda i: (i + begin, 0, 0)),
            row_spec(width),
        ],
        so_far=so_far,
        scratch=[pltpu.VMEM((per_step, GROUP, PAD_COLS, width), BF16)],
        flops=count * TOKENS * width * width * 12,
        through=through,
        vmem=60,
    )


def feed_kernel(count, where, cot, received, x_ref, att_ref, proj_w, proj_b, gain, shift, w1, b1, w2, b2,
                out_kept, grad_mid, grad_att, out_send, o_small, o_b1, o_first, o_second, a_proj,
                padded, placed, pair):
    width = x_ref.shape[1]
    hidden = w1.shape[1]
    step = pl.program_id(0)

    @pl.when(step == 0)
    def _():
        for ref in (padded, o_small, o_b1, pair, a_proj):
            ref[...] = jnp.zeros_like(ref)

    place_rows(where[0], cot, received, padded)
    up = padded[...].reshape(count * TOKENS, width)
    up_f = up.astype(F32)
    up_turned = up.T
    att = att_ref[...]
    middle = x_ref[...].astype(F32) + (dot(att, proj_w[...]) + proj_b[...][None, :])
    hat, inverse = normalise(middle)
    normed = (hat * gain[...][None, :] + shift[...][None, :]).astype(BF16)
    normed_turned = normed.T
    result = middle + b2[...][None, :]
    grad_normed = jnp.zeros((count * TOKENS, width), F32)
    starts = range(0, hidden, FEED_PART)

    def ahead(start):
        cols = slice(start, start + FEED_PART)
        return dot(normed, w1[:, cols]), dot_nt(up, w2[cols, :])

    coming = ahead(0)
    for start in starts:
        cols = slice(start, start + FEED_PART)
        pre_act, grad_act = coming
        if start + FEED_PART < hidden:
            coming = ahead(start + FEED_PART)
        active, slope = gelu_both(pre_act + b1[cols][None, :])
        active = active.astype(BF16)
        grad_pre = grad_act * slope
        o_b1[:, cols] += column_sum(grad_pre)
        grad_pre = grad_pre.astype(BF16)
        result = result + dot(active, w2[cols, :])
        grad_normed = grad_normed + dot_nt(grad_pre, w1[:, cols])
        pair[0, :, cols] += dot(normed_turned, grad_pre)
        pair[1, :, cols] += dot(up_turned, active)
    placed[...] = result.astype(BF16).reshape(placed.shape)
    return_rows(where[0], placed, out_kept, out_send)
    grad_normed = grad_normed.astype(BF16).astype(F32)
    grad_middle = up_f + normalise_back(grad_normed * gain[...][None, :], hat, inverse)
    grad_mid[...] = grad_middle
    branch = grad_middle.astype(BF16)
    a_proj[...] += dot(att.T, branch)
    grad_att[...] = dot_nt(branch, proj_w[...]).astype(BF16)
    o_small[0:1, :] += column_sum(grad_normed * hat)
    o_small[1:2, :] += column_sum(grad_normed)
    o_small[2:3, :] += column_sum(up_f)
    o_small[3:4, :] += column_sum(branch.astype(F32))

    @pl.when(step == pl.num_programs(0) - 1)
    def _():
        core = where[1]
        for part in range(hidden // width):
            cols = slice(part * width, (part + 1) * width)
            o_first[part] = pair[core, :, cols].astype(BF16)
            o_second[part] = pair[1 - core, :, cols].astype(BF16)


def feed(where, cotangent, received, per_step, x, att, weights):
    total, _, cols, width = cotangent.shape
    hidden = weights[4].shape[1]
    rows = per_step * TOKENS
    row_spec = lambda w: pl.BlockSpec((rows, w), lambda i: (i, 0))
    image_spec = lambda n: pl.BlockSpec((per_step, n, cols, width), lambda i: (i, 0, 0, 0))
    accumulated = [
        shaped((8, width), F32),
        shaped((1, hidden), F32),
        shaped((hidden // width, width, width), BF16),
        shaped((hidden // width, width, width), BF16),
        shaped((width, width), F32),
    ]
    return launch(
        partial(feed_kernel, per_step),
        "feed",
        (total // per_step,),
        (where, cotangent, received, x, att, *weights),
        [pl.BlockSpec(memory_space=pltpu.SMEM), image_spec(GROUP), image_spec(SENT), row_spec(width), row_spec(width)]
        + [whole(a.shape) for a in weights],
        [
            shaped((total, GROUP, cols, width), BF16),
            shaped((total * TOKENS, width), F32),
            shaped((total * TOKENS, width), BF16),
            shaped((total, SENT, cols, width), BF16),
        ]
        + accumulated,
        [image_spec(GROUP), row_spec(width), row_spec(width), image_spec(SENT)]
        + [whole(a.shape) for a in accumulated],
        scratch=[
            pltpu.VMEM((per_step, GROUP, PAD_COLS, width), BF16),
            pltpu.VMEM((per_step, GROUP, PAD_COLS, width), BF16),
            pltpu.VMEM((2, width, hidden), F32),
        ],
        flops=total * TOKENS * width * width * 54,
        vmem=60,
    )


def pick_heads(stacked):
    parts = stacked.reshape(PER_BLOCK, TOKENS, LANES)
    lane = lax.broadcasted_iota(jnp.int32, (TOKENS, LANES), 1)
    picked = parts[PER_BLOCK - 1]
    for head in range(PER_BLOCK - 2, -1, -1):
        picked = jnp.where(lane < (head + 1) * HEAD_DIM, parts[head], picked)
    return picked


def back_kernel(count, first_call, last_call, where, normed, qkv, probs_ref, grad_att, mask, a_proj, *refs):
    carried = () if first_call else refs[:3]
    (grads, o_small, o_pair, o_first, o_second, a_w, packed) = refs[len(carried) :]
    width = normed.shape[1]
    step = pl.program_id(0)

    @pl.when(step == 0)
    def _():
        for index, ref in enumerate((o_small, o_pair, a_w)):
            ref[...] = jnp.zeros_like(ref) if first_call else carried[index][...]

    masks = mask[...]
    for two in range(count // 2):
        both = two_images(two)
        for block in range(HEADS // PER_BLOCK):
            at = block * LANES
            here = slice(block * STACK, (block + 1) * STACK)
            query = on_diagonal([qkv[rows, at : at + LANES] for rows in both])
            grad = on_diagonal([grad_att[rows, at : at + LANES] for rows in both])
            vals = side_by_side([qkv[rows, 2 * width + at : 2 * width + at + LANES] for rows in both], masks)
            probs = probs_ref[two, here, :]
            exact = probs.astype(F32).reshape(PER_BLOCK, TOKENS, 2 * LANES)
            grad_probs = dot_nt(vals, grad).reshape(PER_BLOCK, TOKENS, 2 * LANES)
            inner = jnp.sum(grad_probs * exact, axis=1, keepdims=True)
            exact_scores = (exact * (grad_probs - inner)).reshape(STACK, 2 * LANES)
            o_pair[here, :] += exact_scores[:, :LANES] + exact_scores[:, LANES:]
            grad_scores = exact_scores.astype(BF16)
            grad_keys = dot(grad_scores, query)
            grad_vals = dot(probs, grad)
            for half, rows in enumerate(both):
                lanes = slice(half * LANES, (half + 1) * LANES)
                keys = stack_heads(qkv[rows, width + at : width + at + LANES], masks)
                grad_query = dot_tn(grad_scores[:, lanes], keys)[0:TOKENS, :]
                grads[rows, at : at + LANES] = (grad_query * SCALE).astype(BF16)
                grads[rows, width + at : width + at + LANES] = (
                    pick_heads(grad_keys[:, lanes]) * SCALE
                ).astype(BF16)
                grads[rows, 2 * width + at : 2 * width + at + LANES] = pick_heads(grad_vals[:, lanes]).astype(BF16)
    all_grads = grads[...]
    a_w[...] += dot(normed[...].T, all_grads)
    o_small[0:1, :] += column_sum(all_grads[:, :width].astype(F32))
    o_small[1:2, :] += column_sum(all_grads[:, 2 * width :].astype(F32))

    @pl.when(step == pl.num_programs(0) - 1)
    def _():
        if last_call:
            core = where[1]
            for part in range(3):
                packed[part] = a_w[:, part * width : (part + 1) * width].astype(BF16)
            packed[3] = a_proj[...].astype(BF16)
            for part in range(2):
                o_first[part] = packed[2 * core + part]
                o_second[part] = packed[2 - 2 * core + part]
        else:
            o_first[...] = a_w[...]
            o_second[...] = jnp.zeros_like(o_second)


def attend_back(where, first, count, per_step, saved, mask, grad_proj, carried, so_far, last_call, after):
    normed, qkv, probs, grad_att = saved
    width = normed.shape[1]
    begin = first // per_step
    rows = per_step * TOKENS
    extra = () if carried is None else tuple(carried)
    row_spec = lambda w: pl.BlockSpec((rows, w), lambda i: (i + begin, 0))
    fixed = (mask, grad_proj)
    if last_call:
        first_shape = second_shape = shaped((2, width, width), BF16)
    else:
        first_shape = shaped((width, 3 * width), F32)
        second_shape = shaped((8, LANES), F32)
    accumulated = [
        shaped((8, width), F32),
        shaped((HEADS * TOKENS, LANES), F32),
        first_shape,
        second_shape,
    ]
    return launch(
        partial(back_kernel, per_step, carried is None, last_call),
        "attend_back",
        (count // per_step,),
        (where, normed, qkv, probs, grad_att, *fixed, *extra),
        [
            pl.BlockSpec(memory_space=pltpu.SMEM),
            row_spec(width),
            row_spec(3 * width),
            pl.BlockSpec((per_step // 2, HEADS * TOKENS, 2 * LANES), lambda i: (i + begin, 0, 0)),
            row_spec(width),
        ]
        + [whole(a.shape) for a in (*fixed, *extra)],
        [shaped(qkv.shape, BF16)] + accumulated,
        [row_spec(3 * width)] + [whole(a.shape) for a in accumulated],
        so_far=so_far,
        scratch=[
            pltpu.VMEM((width, 3 * width), F32),
            pltpu.VMEM((4, width, width), BF16),
        ],
        flops=count * TOKENS * width * width * 18,
        after=after,
        vmem=60,
    )


def images_kernel(first_call, where, grads, x_ref, grad_mid, gain, weight, *refs):
    carried = () if first_call else refs[:1]
    (gi_kept, gi_send, o_small, placed) = refs[len(carried) :]

    @pl.when(pl.program_id(0) == 0)
    def _():
        o_small[...] = jnp.zeros_like(o_small) if first_call else carried[0][...]

    grad_normed = dot_nt(grads[...], weight[...]).astype(BF16).astype(F32)
    hat, inverse = normalise(x_ref[...].astype(F32))
    o_small[0:1, :] += column_sum(grad_normed * hat)
    o_small[1:2, :] += column_sum(grad_normed)
    grad_image = grad_mid[...] + normalise_back(grad_normed * gain[...][None, :], hat, inverse)
    placed[...] = grad_image.reshape(placed.shape)
    return_rows(where[0], placed, gi_kept, gi_send)


def image_grads(where, first, count, per_step, grads, x, grad_mid, gain, weight, shape, carried, so_far, after):
    total, _, cols, width = shape
    begin = first // per_step
    rows = per_step * TOKENS
    row_spec = lambda w: pl.BlockSpec((rows, w), lambda i: (i + begin, 0))
    fixed = (gain, weight, *carried)
    return launch(
        partial(images_kernel, not carried),
        "image_grads",
        (count // per_step,),
        (where, grads, x, grad_mid, *fixed),
        [pl.BlockSpec(memory_space=pltpu.SMEM), row_spec(3 * width), row_spec(width), row_spec(width)]
        + [whole(a.shape) for a in fixed],
        [
            shaped((total, GROUP, cols, width), F32),
            shaped((count, SENT, cols, width), BF16),
            shaped((8, width), F32),
        ],
        [
            pl.BlockSpec((per_step, GROUP, cols, width), lambda i: (i + begin, 0, 0, 0)),
            pl.BlockSpec((per_step, SENT, cols, width), lambda i: (i, 0, 0, 0)),
            whole((8, width)),
        ],
        so_far=so_far,
        scratch=[pltpu.VMEM((per_step, GROUP, PAD_COLS, width), F32)],
        flops=count * TOKENS * width * width * 6,
        after=after,
        vmem=32,
    )


def swap(value, flip):
    bands, batches = lax.axis_size("band"), lax.axis_size("batch")
    pairs = []
    for band in range(bands):
        for batch in range(batches):
            other = (band ^ flip[0]) * batches + (batch ^ flip[1])
            pairs.append((band * batches + batch, other))
    return lax.ppermute(value, ("band", "batch"), pairs)


def in_plane(value, d):
    return swap(value, (d >> 1, (d & 1) << 1))


PLANE = 4
ALONG = 4


def tree_sum(values):
    while len(values) > 1:
        values = [values[i] + values[i + 1] for i in range(0, len(values), 2)]
    return values[0]


def split_kernel(slot, count, small_rows, where, *refs):
    *refs, token = refs
    token[...] = jnp.zeros_like(token)
    outs = refs[-count - (1 if small_rows else 0) :]
    ins = refs[: len(refs) - len(outs)]
    me = where[slot]
    rows = outs[0].shape[0]
    if small_rows:
        ins, small_ins = ins[:small_rows], ins[small_rows:]
        small = tree_sum([r[...] if r.dtype == F32 else get_pair(r, r.shape[0] - 2 * SMALL) for r in small_ins])

    def total(index):
        start = pl.multiple_of(index * rows, rows)
        return tree_sum([ref[pl.ds(start, rows), :].astype(F32) for ref in ins])

    for d in range(count):
        outs[d][0:rows, :] = total(me ^ d).astype(outs[d].dtype)
        if small_rows and d > 0:
            put_pair(outs[d], rows, small)
    if small_rows:
        high = small.astype(BF16).astype(F32)
        outs[count][...] = high + (small - high).astype(BF16).astype(F32)


def split_share(where, slot, count, values, after, flops=0):
    rows, width = values[0].shape
    size = rows // count
    outs = [shaped((size, width), F32 if d == 0 else BF16) for d in range(count)] + [TOKEN]
    return small_launch(
        partial(split_kernel, slot, count, 0), "split_share", (where, *values), outs, after=after,
        flops=flops,
    )


def split_with_small(where, slot, count, values, smalls, after):
    rows, width = values[0].shape
    size = rows // count
    outs = [shaped((size, width), F32)] + [shaped((size + 2 * SMALL, width), BF16)] * (count - 1)
    outs += [shaped((SMALL, width), F32), TOKEN]
    return small_launch(
        partial(split_kernel, slot, count, len(values)), "split_with_small", (where, *values, *smalls), outs, after=after,
    )


def join_kernel(count, *refs):
    early, late = refs[:count], refs[count : 2 * count]
    small, share, small_out = refs[2 * count :]
    rows, more = early[0].shape[0], late[0].shape[0]
    share[0:rows, :] = tree_sum([r[...].astype(F32) for r in early]).astype(BF16)
    share[rows : rows + more, :] = tree_sum([r[0:more, :].astype(F32) for r in late]).astype(BF16)
    small_out[...] = tree_sum([small[...]] + [get_pair(r, more) for r in late[1:]])


def join_shares(early, late, small, after):
    rows, width = early[0].shape
    return small_launch(
        partial(join_kernel, len(early)),
        "join_shares",
        (*early, *late, small),
        [shaped((rows + late[0].shape[0], width), BF16), shaped((SMALL, width), F32)],
        after=after,
    )


def lay_kernel(slot, where, *refs):
    parts, (small, other, out) = refs[:-3], refs[-3:]
    rows = parts[0].shape[0]
    for d, ref in enumerate(parts):
        out[pl.ds(pl.multiple_of((where[slot] ^ d) * rows, rows), rows), :] = ref[...]
    put_pair(out, len(parts) * rows, small[...] + other[...])


def along(value, d):
    return swap(value, (0, 4 * d))


def spread(pieces, send):
    return [pieces[0]] + [send(piece, d) for d, piece in enumerate(pieces) if d > 0]


def gather_along(where, share, small, after):
    rows, width = share.shape
    parts = spread([share] * ALONG, along)
    return small_launch(
        partial(lay_kernel, 3),
        "lay",
        (where, *parts, small, swap(small, (0, 1))),
        [shaped((ALONG * rows + 2 * SMALL, width), BF16)],
        after=after,
    )[0]


def halve_kernel(across, along_row, low, high):
    low[...] = across[0 : low.shape[0], :]
    high[...] = along_row[low.shape[0] :, :]


def collect_kernel(own, across, along_row, low, high, out, small):
    rows, cut = out.shape[1], low.shape[0]
    out[0] = along_row[0:rows, :]
    out[1] = across[0:rows, :]
    out[2, 0:cut, :] = low[...]
    out[2, cut:rows, :] = high[0 : rows - cut, :]
    far = get_pair(high, rows - cut)
    small[...] = (get_pair(own, rows) + get_pair(along_row, rows)) + (get_pair(across, rows) + far)


def gather_plane(quarter, after):
    theirs = swap(quarter, (0, 1))
    rows, width = quarter.shape
    across, along_row = in_plane(quarter, 2), in_plane(quarter, 1)
    cut = rows // 32 * 16
    low, high = small_launch(
        halve_kernel, "halve", (across, along_row), [shaped((cut, width), BF16), shaped((rows - cut, width), BF16)],
        after=after,
    )
    mine, small = small_launch(
        collect_kernel,
        "collect",
        (quarter, across, along_row, in_plane(low, 1), in_plane(high, 2)),
        [shaped((PLANE - 1, rows - 2 * SMALL, width), BF16), shaped((SMALL, width), F32)],
    )
    return small, (quarter, mine), (theirs, swap(mine, (0, 1)))


def unpack_kernel(flip, early, where, first, rest, o_w1, o_w2, o_qkv, o_proj, feed_buf, att_buf, sems):
    me, side = where[2], where[1] ^ flip
    width = o_proj.shape[0]
    late = width // 2 // ALONG
    low, high = slice(0, width // 2), slice(width // 2, width)
    def quarter_of(d):
        return first if d == 0 else rest.at[d - 1]

    def place(d):
        return pl.ds(pl.multiple_of((me ^ d) * width, width), width)

    for d in range(PLANE):
        for share in range(ALONG):
            start = share * (early + late) + early
            att_buf[me ^ d, share * late : (share + 1) * late, :] = quarter_of(d)[start : start + late, :].astype(F32)

    def run(att_targets, feed_target, turned):
        copies = []
        for index, (target, rows, cols) in enumerate(att_targets):
            copies.append(pltpu.make_async_copy(att_buf.at[index], target.at[rows, cols], sems.at[len(copies)]))
            copies[-1].start()
        for d in range(PLANE):
            shares = [quarter_of(d)[i * (early + late) : i * (early + late) + early, :] for i in range(ALONG)]
            block = jnp.concatenate(shares, axis=0).astype(F32)
            feed_buf[d] = block.T if turned else block
            copies.append(pltpu.make_async_copy(feed_buf.at[d], feed_target(d), sems.at[len(copies)]))
            copies[-1].start()
        for copy in copies:
            copy.wait()

    def halves(target, cols):
        return [(target, low, cols), (target, high, cols)]

    @pl.when(side == 0)
    def _():
        targets = halves(o_qkv, slice(0, width)) + halves(o_qkv, slice(width, 2 * width))
        run(targets, lambda d: o_w1.at[:, place(d)], False)

    @pl.when(side == 1)
    def _():
        targets = halves(o_qkv, slice(2 * width, 3 * width)) + halves(o_proj, slice(0, width))
        run(targets, lambda d: o_w2.at[place(d), :], True)


def unpack(flip, early, where, half, shapes, so_far):
    width = half[0].shape[1]
    vector = pl.BlockSpec(memory_space=pltpu.VMEM)
    return launch(
        partial(unpack_kernel, flip, early),
        "unpack",
        (),
        (where, *half),
        [pl.BlockSpec(memory_space=pltpu.SMEM), vector, vector],
        [shaped(shape, F32) for shape in shapes],
        [pl.BlockSpec(memory_space=pl.ANY)] * len(shapes),
        so_far=so_far,
        scratch=[
            pltpu.VMEM((PLANE, width, width), F32),
            pltpu.VMEM((PLANE, width // 2, width), F32),
            pltpu.SemaphoreType.DMA((2 * PLANE,)),
        ],
        vmem=24,
    )


def body(images, cotangent, norm1_gain, norm1_shift, qkv_weight, qv_bias, proj_weight, proj_bias, *rest):
    pos = rest[:13]
    norm2_gain, norm2_shift, fc1_weight, fc1_bias, fc2_weight, fc2_bias = rest[13:]
    total, _, cols, width = images.shape
    hidden = fc1_weight.shape[1]
    per_step = 4
    band, batch = lax.axis_index("band"), lax.axis_index("batch")
    where = jnp.stack([band, batch % 2, band * 2 + batch // 2 % 2, batch // 4 % ALONG]).astype(jnp.int32)
    head_of_row = np.arange(STACK)[:, None] // TOKENS
    mask = jnp.asarray(head_of_row == np.arange(LANES)[None, :] // HEAD_DIM, BF16)
    to_partner = lambda value: swap(value, (1, 0))
    pos = (*pos[:12], pos[12].T)

    later = (total // per_step * 2 // 5) * per_step
    image_chunks = [(0, later), (later, total - later)]
    packed, token = pack_rows((images,), [(0, *image_chunks[0])])
    received = to_partner(packed)
    later_packed, cot_packed, _ = pack_rows(
        (images, cotangent), [(0, *image_chunks[1]), (1, 0, total)], (token,)
    )
    pair, later_packed, cot_packed = pair_bias(pos, (later_packed, cot_packed))
    later_received = to_partner(later_packed)
    norm_one = (norm1_gain, norm1_shift, qkv_weight, qv_bias, pair, mask)
    so_far = attend(where, images, received, 0, per_step, *norm_one, (), ())
    _, cot_packed = small_launch(
        token_kernel, "order", (), [TOKEN], after=(*so_far[:1], later_received), vmem=60, through=(cot_packed,)
    )
    cot_rows = to_partner(cot_packed)
    so_far = attend(where, images, later_received, later, per_step, *norm_one, so_far, ())
    x, normed, qkv, probs, att = so_far
    weights = (proj_weight, proj_bias, norm2_gain, norm2_shift, fc1_weight, fc1_bias, fc2_weight, fc2_bias)
    result = feed(where, cotangent, cot_rows, per_step, x, att, weights)
    out_images, grad_mid, grad_att, out_sent, feed_small, feed_b1, mine, theirs, grad_proj = result
    out_rows = to_partner(out_sent)
    flat = lambda value: value.reshape(-1, width)
    early = [flat(mine), swap(flat(theirs), (0, 1))]

    saved = (normed, qkv, probs, grad_att)
    chunks = [(0, total - later), (total - later, later)]
    result = attend_back(where, *chunks[0], per_step, saved, mask, grad_proj, None, (), False, ())
    *pieces, token = split_share(where, 2, PLANE, early, (result[1],))
    early = spread(pieces, in_plane)
    result = attend_back(where, *chunks[1], per_step, saved, mask, grad_proj, result[1:4], result[:1], True,
                         (token, out_rows))
    grads, att_small, grad_pair = result[:3]
    mine, theirs = flat(result[3]), flat(result[4])
    *pieces, token = split_share(where, 3, ALONG, early, (att_small,), 5e9)
    early = spread(pieces, along)
    *pieces, token = split_share(where, 2, PLANE, [mine, swap(theirs, (0, 1))], (token,))
    late = spread(pieces, in_plane)
    grad_images, sent, norm_small = image_grads(where, 0, total, per_step, grads, x, grad_mid, norm1_gain,
                                                qkv_weight, images.shape, (), (), (token,))
    grad_rows = to_partner(sent)
    small = gather_small(feed_small, feed_b1, att_small, norm_small, grad_pair)
    *pieces, small, _ = split_with_small(where, 3, ALONG, late, [small], early[1:])
    late = spread(pieces, along)
    share, small = join_shares(early, late, small, ())
    stride = PLANE * ALONG
    while stride < lax.axis_size("batch"):
        share = (share.astype(F32) + swap(share, (0, stride)).astype(F32)).astype(BF16)
        small = small + swap(small, (0, stride))
        stride *= 2
    out_images, token = merge_rows(out_rows, out_images, 0)
    quarter = gather_along(where, share, small, (token,))
    grad_images, token = merge_rows(grad_rows, grad_images, 0)
    small, half, other_half = gather_plane(quarter, (token,))
    smalls = finish_small(pos, small, hidden)
    shapes = [w.shape for w in (fc1_weight, fc2_weight, qkv_weight, proj_weight)]
    large = unpack(0, early[0].shape[0], where, half, shapes, ())
    grad_fc1, grad_fc2, grad_qkv, grad_proj = unpack(1, early[0].shape[0], where, other_half, shapes, large)
    n1_gain, n1_shift, qv, proj_b, n2_gain, n2_shift, fc1_b, fc2_b = smalls[:8]
    return (out_images, grad_images, n1_gain, n1_shift, grad_qkv, qv, grad_proj, proj_b, *smalls[8:20], smalls[20].T,
            n2_gain, n2_shift, grad_fc1, fc1_b, grad_fc2, fc2_b)


def solution(mesh):
    tokens = P("batch", "band", None, None)
    return jax.shard_map(
        body,
        mesh=mesh,
        in_specs=(tokens, tokens) + (P(),) * 25,
        out_specs=(tokens, tokens) + (P(),) * 25,
        check_vma=False,
    )
```

```python
import math
from functools import partial

import jax
import jax.numpy as jnp
import numpy as np
from jax import lax
from jax.experimental import pallas as pl
from jax.experimental.pallas import tpu as pltpu
from jax.sharding import PartitionSpec as P

HEADS = 12
GROUP = 7
HEAD_DIM = 32
SPAN = 2 * GROUP - 1
HIGH = lax.Precision.HIGHEST
EPSILON = 1e-05
SCALE = HEAD_DIM**-0.5
MASKED = -1e30
PAD_COLS = 16
TOKENS = GROUP * PAD_COLS
LANES = 128
PER_BLOCK = LANES // HEAD_DIM
STACK = PER_BLOCK * TOKENS
KEPT = (GROUP + 1) // 2
SENT = GROUP - KEPT
OFFSETS = 176
WIDE = SPAN * PAD_COLS
F32 = jnp.float32
BF16 = jnp.bfloat16


def dot(a, b, precision=None):
    return lax.dot_general(a, b, (((1,), (0,)), ((), ())), precision=precision, preferred_element_type=F32)


def dot_nt(a, b, precision=None):
    return lax.dot_general(a, b, (((1,), (1,)), ((), ())), precision=precision, preferred_element_type=F32)


def dot_tn(a, b, precision=None):
    return lax.dot_general(a, b, (((0,), (0,)), ((), ())), precision=precision, preferred_element_type=F32)


def whole(shape):
    zeros = (0,) * len(shape)
    return pl.BlockSpec(shape, lambda *_: zeros, pipeline_mode=pl.Buffered(1))


def normalise(values):
    mean = jnp.mean(values, axis=-1, keepdims=True)
    centred = values - mean
    inverse = lax.rsqrt(jnp.mean(centred * centred, axis=-1, keepdims=True) + EPSILON)
    return centred * inverse, inverse


def normalise_back(grad_hat, hat, inverse):
    first = jnp.mean(grad_hat, axis=-1, keepdims=True)
    second = jnp.mean(grad_hat * hat, axis=-1, keepdims=True)
    return inverse * (grad_hat - first - hat * second)


def gelu_both(v):
    cdf = 0.5 + 0.5 * lax.erf(v * (0.5**0.5))
    density = jnp.exp(-0.5 * v * v) * ((2.0 * np.pi) ** -0.5)
    return v * cdf, cdf + v * density


def column_sum(values):
    return jnp.sum(values, axis=0, keepdims=True)


SMALL = 24


ROWS = 32


def by_rows(function, *arrays):
    parts = [
        function(*(array[start : start + ROWS, :] for array in arrays))
        for start in range(0, arrays[0].shape[0], ROWS)
    ]
    return tuple(jnp.concatenate(part, axis=0) for part in zip(*parts))


def by_eights(values):
    return jnp.sum(values.reshape(values.shape[0] // 8, 8, values.shape[1]), axis=0)


def launch(kernel, name, grid, inputs, in_specs, out_shape, out_specs, so_far=(), scratch=(), flops=0,
           after=(), vmem=16, through=()):
    count, held = len(inputs), len(so_far) + len(after) + len(through)
    own = len(out_shape)
    hand = {count + len(so_far) + len(after) + i: own + i for i in range(len(through))}
    inner = kernel
    if held:
        kernel = lambda *refs: inner(
            *refs[:count], *refs[count + held : count + held + own], *refs[count + held + own + len(through) :]
        )
    moved = sum(a.size * a.dtype.itemsize for a in (*inputs, *out_shape))
    return pl.pallas_call(
        kernel,
        grid=grid,
        in_specs=list(in_specs) + [pl.BlockSpec(memory_space=pl.ANY)] * held,
        out_specs=list(out_specs) + [pl.BlockSpec(memory_space=pl.ANY)] * len(through),
        out_shape=list(out_shape) + [shaped(a.shape, a.dtype) for a in through],
        input_output_aliases={count + i: i for i in range(len(so_far))} | hand,
        scratch_shapes=list(scratch),
        compiler_params=pltpu.CompilerParams(vmem_limit_bytes=vmem * 2**20),
        cost_estimate=pl.CostEstimate(flops=int(flops), bytes_accessed=int(moved), transcendentals=0),
        name=name,
    )(*inputs, *so_far, *after, *through)


def small_launch(kernel, name, inputs, out_shape, scratch=(), flops=0, after=(), vmem=16, through=()):
    specs = [pl.BlockSpec(memory_space=pltpu.SMEM if a.dtype == jnp.int32 else pltpu.VMEM) for a in inputs]
    outs = [pl.BlockSpec(memory_space=pltpu.VMEM)] * len(out_shape)
    return launch(kernel, name, (), inputs, specs, out_shape, outs, scratch=scratch, flops=flops, after=after, vmem=vmem,
                  through=through)


def shaped(shape, dtype):
    return jax.ShapeDtypeStruct(shape, dtype)


FEED_PART = 512
TOKEN = shaped((8, LANES), F32)


def token_kernel(token):
    token[...] = jnp.zeros_like(token)


def merge_kernel(source, target, token):
    target[...] = source[...].astype(target.dtype)
    token[...] = jnp.zeros_like(token)


def pack_kernel(pieces, *refs):
    count = 1 + max(piece[0] for piece in pieces)
    sources, outs, (token, sems) = refs[:count], refs[count:-2], refs[-2:]
    token[...] = jnp.zeros_like(token)
    copies = []
    for (source, first, images), out in zip(pieces, outs):
        for row in range(SENT):
            copies.append(
                pltpu.make_async_copy(
                    sources[source].at[first : first + images, 2 * row + 1], out.at[:, row], sems.at[len(copies)]
                )
            )
    for copy in copies:
        copy.start()
    for copy in copies:
        copy.wait()


def pack_rows(sources, pieces, after=()):
    _, _, cols, width = sources[0].shape
    vector = pl.BlockSpec(memory_space=pltpu.VMEM)
    return launch(
        partial(pack_kernel, pieces),
        "pack_rows",
        (),
        sources,
        [pl.BlockSpec(memory_space=pl.ANY)] * len(sources),
        [shaped((count, SENT, cols, width), BF16) for _, _, count in pieces] + [TOKEN],
        [vector] * (len(pieces) + 1),
        scratch=[pltpu.SemaphoreType.DMA((SENT * len(pieces),))],
        after=after,
        vmem=60,
    )


def merge_rows(received, target, first):
    count, _, cols, width = received.shape
    unit = math.gcd(first, count)
    begin = first // unit
    return launch(
        merge_kernel,
        "merge_rows",
        (count // unit, SENT),
        (received,),
        [pl.BlockSpec((unit, 1, cols, width), lambda i, r: (i, r, 0, 0))],
        [shaped(target.shape, target.dtype), TOKEN],
        [pl.BlockSpec((unit, 1, cols, width), lambda i, r: (i + begin, 2 * r + 1, 0, 0)), whole(TOKEN.shape)],
        so_far=(target,),
    )


def position_layers(refs):
    (in_w, in_b, g1, s1, w1, b1, g2, s2, w2, b2, g3, s3, _) = refs
    width = in_w.shape[1]
    offset = lax.broadcasted_iota(jnp.int32, (OFFSETS, width), 0)
    rows = (offset // SPAN - (GROUP - 1)).astype(F32)
    cols = (offset % SPAN - (GROUP - 1)).astype(F32)
    hidden = rows * in_w[0:1, :] + cols * in_w[1:2, :] + in_b[...][None, :]
    kept = []
    for gain, shift, weight, bias in ((g1, s1, w1, b1), (g2, s2, w2, b2), (g3, s3, None, None)):
        hat, inverse = normalise(hidden)
        active, slope = gelu_both(hat * gain[...][None, :] + shift[...][None, :])
        kept.append((hat, inverse, active, slope))
        if weight is not None:
            hidden = dot(active, weight[...], HIGH) + bias[...][None, :]
    return rows, cols, kept


def pick_offsets(place):
    offset = lax.broadcasted_iota(jnp.int32, (OFFSETS, WIDE), 0)
    lane = lax.broadcasted_iota(jnp.int32, (OFFSETS, WIDE), 1)
    wanted = lane // PAD_COLS * SPAN + lane % PAD_COLS // 2 - place + GROUP - 1
    return jnp.where(offset == wanted, 1.0, 0.0).astype(F32)


def bias_kernel(*refs):
    ins, (out, strip) = refs[:13], refs[13:]
    _, _, kept = position_layers(ins)
    table = dot_nt(ins[12][...], kept[2][2], HIGH)
    lane = lax.broadcasted_iota(jnp.int32, (HEADS, WIDE), 1)
    even = lane % 2 == 0
    strip[...] = jnp.full(strip.shape, MASKED, F32)
    for place in range(GROUP):
        spread = dot(table, pick_offsets(place), HIGH)
        strip[:, 2 * place, 0:WIDE] = jnp.where(even, spread, MASKED)
        strip[:, 2 * place + 1, 0:WIDE] = jnp.where(even, MASKED, spread)
    out[...] = jnp.zeros_like(out)
    for row in range(GROUP):
        start = (GROUP - 1 - row) * PAD_COLS
        out[:, row * PAD_COLS : (row + 1) * PAD_COLS, 0:TOKENS] = strip[:, :, start : start + TOKENS]


def pair_bias(pos, through):
    return small_launch(
        bias_kernel,
        "pair_bias",
        pos,
        [shaped((HEADS, TOKENS, LANES), F32)],
        [pltpu.VMEM((HEADS, PAD_COLS, 2 * LANES), F32)],
        through=through,
        vmem=60,
    )


def put_pair(ref, start, values):
    high = values.astype(BF16)
    ref[start : start + SMALL, :] = high
    ref[start + SMALL : start + 2 * SMALL, :] = (values - high.astype(F32)).astype(BF16)


def get_pair(ref, start):
    return ref[start : start + SMALL, :].astype(F32) + ref[start + SMALL : start + 2 * SMALL, :].astype(F32)


def gather_small_kernel(feed_small, feed_b1, att_small, norm_small, grad_pair, out, small):
    width = feed_small.shape[1]
    strip = jnp.zeros((HEADS, PAD_COLS, WIDE), F32)
    for row in range(GROUP):
        start = (GROUP - 1 - row) * PAD_COLS
        piece = grad_pair[:, row * PAD_COLS : (row + 1) * PAD_COLS, 0:TOKENS]
        strip = strip + jnp.pad(piece, ((0, 0), (0, 0), (start, WIDE - start - TOKENS)))
    table = jnp.zeros((HEADS, OFFSETS), F32)
    for place in range(GROUP):
        folded = strip[:, 2 * place, :] + strip[:, 2 * place + 1, :]
        table = table + dot_nt(folded, pick_offsets(place), HIGH)
    small[...] = jnp.zeros_like(small)
    small[0:4, :] = feed_small[0:4, :]
    small[4:6, :] = norm_small[0:2, :]
    small[6:8, :] = att_small[0:2, :]
    for part in range(feed_b1.shape[1] // width):
        small[8 + part : 9 + part, :] = feed_b1[:, part * width : (part + 1) * width]
    small[12 : 12 + HEADS, 0:OFFSETS] = table
    put_pair(out, 0, small[...])


def gather_small(feed_small, feed_b1, att_small, norm_small, grad_pair):
    width = feed_small.shape[1]
    return small_launch(
        gather_small_kernel,
        "gather_small",
        (feed_small, feed_b1, att_small, norm_small, grad_pair.reshape(HEADS, TOKENS, LANES)),
        [shaped((2 * SMALL, width), BF16)],
        [pltpu.VMEM((SMALL, width), F32)],
    )[0]


def finish_small_kernel(*refs):
    ins, small, outs, token = refs[:13], refs[13], refs[14:-1], refs[-1]
    token[...] = jnp.zeros_like(token)
    (in_w, in_b, g1, s1, w1, b1, g2, s2, w2, b2, g3, s3, w3) = ins
    (o_n1_gain, o_n1_shift, o_qv, o_proj_b, o_n2_gain, o_n2_shift, o_fc1_b, o_fc2_b) = outs[:8]
    (o_in_w, o_in_b, o_g1, o_s1, o_w1, o_b1, o_g2, o_s2, o_w2, o_b2, o_g3, o_s3, o_w3) = outs[8:]
    o_n2_gain[...] = small[0, :]
    o_n2_shift[...] = small[1, :]
    o_fc2_b[...] = small[2, :]
    o_proj_b[...] = small[3, :]
    o_n1_gain[...] = small[4, :]
    o_n1_shift[...] = small[5, :]
    o_qv[...] = small[6:8, :]
    width = small.shape[1]
    for part in range(o_fc1_b.shape[0] // width):
        o_fc1_b[part * width : (part + 1) * width] = small[8 + part, :]
    rows, cols, kept = position_layers(ins)
    table = small[12 : 12 + HEADS, 0:OFFSETS]
    o_w3[...] = dot(table, kept[2][2], HIGH)
    grad_active = dot(table.T, w3[...], HIGH)
    stages = (
        (g3, o_g3, o_s3, o_b2, o_w2, w2),
        (g2, o_g2, o_s2, o_b1, o_w1, w1),
        (g1, o_g1, o_s1, o_in_b, None, None),
    )
    for level, (gain, o_gain, o_shift, o_bias, o_weight, weight) in zip((2, 1, 0), stages):
        hat, inverse, _, slope = kept[level]
        grad_norm = grad_active * slope
        o_gain[...] = jnp.sum(grad_norm * hat, axis=0)
        o_shift[...] = jnp.sum(grad_norm, axis=0)
        grad_hidden = normalise_back(grad_norm * gain[...][None, :], hat, inverse)
        o_bias[...] = jnp.sum(grad_hidden, axis=0)
        if weight is not None:
            o_weight[...] = dot(kept[level - 1][2].T, grad_hidden, HIGH)
            grad_active = dot_nt(grad_hidden, weight[...], HIGH)
        else:
            o_in_w[0:1, :] = column_sum(grad_hidden * rows)
            o_in_w[1:2, :] = column_sum(grad_hidden * cols)


def finish_small(pos, small, hidden):
    width = small.shape[1]
    shapes = [(width,), (width,), (2, width), (width,), (width,), (width,), (hidden,), (width,)]
    return small_launch(
        finish_small_kernel,
        "finish_small",
        (*pos, small),
        [shaped(s, F32) for s in shapes] + [shaped(p.shape, F32) for p in pos] + [TOKEN],
    )


def stack_heads(block, mask):
    return jnp.concatenate([block] * PER_BLOCK, axis=0) * mask


def head_rows(head, start=0):
    return slice(start + head * TOKENS, start + (head + 1) * TOKENS)


def half_lanes(half):
    return slice(half * LANES, (half + 1) * LANES)


def two_images(two):
    return [slice(image * TOKENS, (image + 1) * TOKENS) for image in (2 * two, 2 * two + 1)]


def on_diagonal(blocks):
    rest = jnp.zeros((LANES - TOKENS, LANES), BF16)
    zero = jnp.zeros((LANES, LANES), BF16)
    first, second = [jnp.concatenate([block, rest], axis=0) for block in blocks]
    return jnp.concatenate(
        [jnp.concatenate([first, zero], axis=1), jnp.concatenate([zero, second], axis=1)], axis=0
    )


def side_by_side(blocks, mask):
    return jnp.concatenate([stack_heads(block, mask) for block in blocks], axis=1)


def place_rows(band, kept_ref, received_ref, padded):
    upper = band * SENT
    lower = (1 - band) * KEPT
    for row in range(KEPT):
        padded[:, row + upper, 0 : 2 * GROUP, :] = kept_ref[:, 2 * row]
    for row in range(SENT):
        padded[:, row + lower, 0 : 2 * GROUP, :] = received_ref[:, row]


def return_rows(band, placed, kept_ref, sent_ref):
    upper = band * SENT
    lower = (1 - band) * KEPT
    for row in range(KEPT):
        kept_ref[:, 2 * row] = placed[:, row + upper, 0 : 2 * GROUP, :]
    for row in range(SENT):
        sent_ref[:, row] = placed[:, row + lower, 0 : 2 * GROUP, :].astype(sent_ref.dtype)


def attend_kernel(count, where, images, received, gain, shift, weight, bias, pair, mask,
                  x_out, normed_out, qkv_out, probs_out, att_out, padded):
    width = images.shape[3]

    @pl.when(pl.program_id(0) == 0)
    def _():
        padded[...] = jnp.zeros_like(padded)

    place_rows(where[0], images, received, padded)
    x = padded[...].reshape(count * TOKENS, width)
    x_out[...] = x
    gains, shifts = gain[...][None, :], shift[...][None, :]
    (normed,) = by_rows(lambda v: ((normalise(v.astype(F32))[0] * gains + shifts).astype(BF16),), x)
    normed_out[...] = normed
    piece = dot(normed, weight[...])
    qkv_out[:, 0:width] = (piece[:, 0:width] + bias[0:1, :]).astype(BF16)
    qkv_out[:, width : 2 * width] = piece[:, width : 2 * width].astype(BF16)
    qkv_out[:, 2 * width :] = (piece[:, 2 * width :] + bias[1:2, :]).astype(BF16)
    masks = mask[...]
    for two in range(count // 2):
        both = two_images(two)
        for block in range(HEADS // PER_BLOCK):
            at = block * LANES
            here = slice(block * STACK, (block + 1) * STACK)
            query = on_diagonal([qkv_out[rows, at : at + LANES] for rows in both])
            keys = side_by_side([qkv_out[rows, width + at : width + at + LANES] for rows in both], masks)
            scores = dot_nt(keys, query)
            probs = []
            for head in range(PER_BLOCK):
                bias_here = pair[head_rows(head, block * STACK), :]
                halves = []
                for half in range(2):
                    values = scores[head_rows(head), half_lanes(half)] * SCALE + bias_here
                    values = jnp.exp(values - jnp.max(values, axis=0, keepdims=True))
                    values = values * (1.0 / jnp.sum(values, axis=0, keepdims=True))
                    halves.append(values.astype(BF16))
                probs.append(jnp.concatenate(halves, axis=1))
            probs = jnp.concatenate(probs, axis=0)
            probs_out[two, here, :] = probs
            for half, rows in enumerate(both):
                vals = stack_heads(qkv_out[rows, 2 * width + at : 2 * width + at + LANES], masks)
                attended = dot_tn(probs[:, half * LANES : (half + 1) * LANES], vals)
                att_out[rows, at : at + LANES] = attended[0:TOKENS, :].astype(BF16)


def attend(where, images, received, first, per_step, gain, shift, weight, bias, pair, mask, so_far, through):
    total, _, cols, width = images.shape
    count = received.shape[0]
    begin = first // per_step
    rows = per_step * TOKENS
    row_spec = lambda w: pl.BlockSpec((rows, w), lambda i: (i + begin, 0))
    fixed = (gain, shift, weight, bias, pair.reshape(HEADS * TOKENS, LANES), mask)
    return launch(
        partial(attend_kernel, per_step),
        "attend",
        (count // per_step,),
        (where, images, received, *fixed),
        [
            pl.BlockSpec(memory_space=pltpu.SMEM),
            pl.BlockSpec((per_step, GROUP, cols, width), lambda i: (i + begin, 0, 0, 0)),
            pl.BlockSpec((per_step, SENT, cols, width), lambda i: (i, 0, 0, 0)),
        ]
        + [whole(a.shape) for a in fixed],
        [
            shaped((total * TOKENS, width), BF16),
            shaped((total * TOKENS, width), BF16),
            shaped((total * TOKENS, 3 * width), BF16),
            shaped((total // 2, HEADS * TOKENS, 2 * LANES), BF16),
            shaped((total * TOKENS, width), BF16),
        ],
        [
            row_spec(width),
            row_spec(width),
            row_spec(3 * width),
            pl.BlockSpec((per_step // 2, HEADS * TOKENS, 2 * LANES), lambda i: (i + begin, 0, 0)),
            row_spec(width),
        ],
        so_far=so_far,
        scratch=[pltpu.VMEM((per_step, GROUP, PAD_COLS, width), BF16)],
        flops=count * TOKENS * width * width * 12,
        through=through,
        vmem=60,
    )


def feed_kernel(count, where, cot, received, x_ref, att_ref, proj_w, proj_b, gain, shift, w1, b1, w2, b2,
                out_kept, grad_mid, grad_att, out_send, o_small, o_b1, o_first, o_second, a_proj,
                padded, placed, pair):
    width = x_ref.shape[1]
    hidden = w1.shape[1]
    step = pl.program_id(0)

    @pl.when(step == 0)
    def _():
        for ref in (padded, o_small, o_b1, pair, a_proj):
            ref[...] = jnp.zeros_like(ref)

    place_rows(where[0], cot, received, padded)
    up = padded[...].reshape(count * TOKENS, width)
    up_f = up.astype(F32)
    up_turned = up.T
    att = att_ref[...]
    middle = x_ref[...].astype(F32) + (dot(att, proj_w[...]) + proj_b[...][None, :])
    hat, inverse = normalise(middle)
    normed = (hat * gain[...][None, :] + shift[...][None, :]).astype(BF16)
    normed_turned = normed.T
    result = middle + b2[...][None, :]
    grad_normed = jnp.zeros((count * TOKENS, width), F32)
    starts = range(0, hidden, FEED_PART)

    def ahead(start):
        cols = slice(start, start + FEED_PART)
        return dot(normed, w1[:, cols]), dot_nt(up, w2[cols, :])

    coming = ahead(0)
    for start in starts:
        cols = slice(start, start + FEED_PART)
        pre_act, grad_act = coming
        if start + FEED_PART < hidden:
            coming = ahead(start + FEED_PART)
        active, slope = gelu_both(pre_act + b1[cols][None, :])
        active = active.astype(BF16)
        grad_pre = grad_act * slope
        o_b1[:, cols] += column_sum(grad_pre)
        grad_pre = grad_pre.astype(BF16)
        result = result + dot(active, w2[cols, :])
        grad_normed = grad_normed + dot_nt(grad_pre, w1[:, cols])
        pair[0, :, cols] += dot(normed_turned, grad_pre)
        pair[1, :, cols] += dot(up_turned, active)
    placed[...] = result.astype(BF16).reshape(placed.shape)
    return_rows(where[0], placed, out_kept, out_send)
    grad_normed = grad_normed.astype(BF16).astype(F32)
    grad_middle = up_f + normalise_back(grad_normed * gain[...][None, :], hat, inverse)
    grad_mid[...] = grad_middle
    branch = grad_middle.astype(BF16)
    a_proj[...] += dot(att.T, branch)
    grad_att[...] = dot_nt(branch, proj_w[...]).astype(BF16)
    o_small[0:1, :] += column_sum(grad_normed * hat)
    o_small[1:2, :] += column_sum(grad_normed)
    o_small[2:3, :] += column_sum(up_f)
    o_small[3:4, :] += column_sum(branch.astype(F32))

    @pl.when(step == pl.num_programs(0) - 1)
    def _():
        core = where[1]
        for part in range(hidden // width):
            cols = slice(part * width, (part + 1) * width)
            o_first[part] = pair[core, :, cols].astype(BF16)
            o_second[part] = pair[1 - core, :, cols].astype(BF16)


def feed(where, cotangent, received, per_step, x, att, weights):
    total, _, cols, width = cotangent.shape
    hidden = weights[4].shape[1]
    rows = per_step * TOKENS
    row_spec = lambda w: pl.BlockSpec((rows, w), lambda i: (i, 0))
    image_spec = lambda n: pl.BlockSpec((per_step, n, cols, width), lambda i: (i, 0, 0, 0))
    accumulated = [
        shaped((8, width), F32),
        shaped((1, hidden), F32),
        shaped((hidden // width, width, width), BF16),
        shaped((hidden // width, width, width), BF16),
        shaped((width, width), F32),
    ]
    return launch(
        partial(feed_kernel, per_step),
        "feed",
        (total // per_step,),
        (where, cotangent, received, x, att, *weights),
        [pl.BlockSpec(memory_space=pltpu.SMEM), image_spec(GROUP), image_spec(SENT), row_spec(width), row_spec(width)]
        + [whole(a.shape) for a in weights],
        [
            shaped((total, GROUP, cols, width), BF16),
            shaped((total * TOKENS, width), F32),
            shaped((total * TOKENS, width), BF16),
            shaped((total, SENT, cols, width), BF16),
        ]
        + accumulated,
        [image_spec(GROUP), row_spec(width), row_spec(width), image_spec(SENT)]
        + [whole(a.shape) for a in accumulated],
        scratch=[
            pltpu.VMEM((per_step, GROUP, PAD_COLS, width), BF16),
            pltpu.VMEM((per_step, GROUP, PAD_COLS, width), BF16),
            pltpu.VMEM((2, width, hidden), F32),
        ],
        flops=total * TOKENS * width * width * 54,
        vmem=60,
    )


def pick_heads(stacked):
    parts = stacked.reshape(PER_BLOCK, TOKENS, LANES)
    lane = lax.broadcasted_iota(jnp.int32, (TOKENS, LANES), 1)
    picked = parts[PER_BLOCK - 1]
    for head in range(PER_BLOCK - 2, -1, -1):
        picked = jnp.where(lane < (head + 1) * HEAD_DIM, parts[head], picked)
    return picked


def back_kernel(count, first_call, last_call, where, normed, qkv, probs_ref, grad_att, mask, a_proj, *refs):
    carried = () if first_call else refs[:3]
    (grads, o_small, o_pair, o_first, o_second, a_w, packed) = refs[len(carried) :]
    width = normed.shape[1]
    step = pl.program_id(0)

    @pl.when(step == 0)
    def _():
        for index, ref in enumerate((o_small, o_pair, a_w)):
            ref[...] = jnp.zeros_like(ref) if first_call else carried[index][...]

    masks = mask[...]
    for two in range(count // 2):
        both = two_images(two)
        for block in range(HEADS // PER_BLOCK):
            at = block * LANES
            here = slice(block * STACK, (block + 1) * STACK)
            query = on_diagonal([qkv[rows, at : at + LANES] for rows in both])
            grad = on_diagonal([grad_att[rows, at : at + LANES] for rows in both])
            vals = side_by_side([qkv[rows, 2 * width + at : 2 * width + at + LANES] for rows in both], masks)
            probs = probs_ref[two, here, :]
            grad_probs = dot_nt(vals, grad)
            grad_scores = []
            for head in range(PER_BLOCK):
                halves, total = [], None
                for half in range(2):
                    exact = probs[head_rows(head), half_lanes(half)].astype(F32)
                    values = grad_probs[head_rows(head), half_lanes(half)]
                    inner = jnp.sum(values * exact, axis=0, keepdims=True)
                    values = exact * (values - inner)
                    total = values if total is None else total + values
                    halves.append(values.astype(BF16))
                o_pair[head_rows(head, block * STACK), :] += total
                grad_scores.append(jnp.concatenate(halves, axis=1))
            grad_scores = jnp.concatenate(grad_scores, axis=0)
            grad_keys = dot(grad_scores, query)
            grad_vals = dot(probs, grad)
            for half, rows in enumerate(both):
                lanes = slice(half * LANES, (half + 1) * LANES)
                keys = stack_heads(qkv[rows, width + at : width + at + LANES], masks)
                grad_query = dot_tn(grad_scores[:, lanes], keys)[0:TOKENS, :]
                grads[rows, at : at + LANES] = (grad_query * SCALE).astype(BF16)
                grads[rows, width + at : width + at + LANES] = (
                    pick_heads(grad_keys[:, lanes]) * SCALE
                ).astype(BF16)
                grads[rows, 2 * width + at : 2 * width + at + LANES] = pick_heads(grad_vals[:, lanes]).astype(BF16)
    all_grads = grads[...]
    a_w[...] += dot(normed[...].T, all_grads)
    sums = [jnp.zeros((8, width), F32)] * 2
    for start in range(0, count * TOKENS, ROWS):
        piece = grads[start : start + ROWS, :]
        sums[0] = sums[0] + by_eights(piece[:, :width].astype(F32))
        sums[1] = sums[1] + by_eights(piece[:, 2 * width :].astype(F32))
    o_small[0:1, :] += column_sum(sums[0])
    o_small[1:2, :] += column_sum(sums[1])

    @pl.when(step == pl.num_programs(0) - 1)
    def _():
        if last_call:
            core = where[1]
            for part in range(3):
                packed[part] = a_w[:, part * width : (part + 1) * width].astype(BF16)
            packed[3] = a_proj[...].astype(BF16)
            for part in range(2):
                o_first[part] = packed[2 * core + part]
                o_second[part] = packed[2 - 2 * core + part]
        else:
            o_first[...] = a_w[...]
            o_second[...] = jnp.zeros_like(o_second)


def attend_back(where, first, count, per_step, saved, mask, grad_proj, carried, so_far, last_call, after, through):
    normed, qkv, probs, grad_att = saved
    width = normed.shape[1]
    begin = first // per_step
    rows = per_step * TOKENS
    extra = () if carried is None else tuple(carried)
    row_spec = lambda w: pl.BlockSpec((rows, w), lambda i: (i + begin, 0))
    fixed = (mask, grad_proj)
    if last_call:
        first_shape = second_shape = shaped((2, width, width), BF16)
    else:
        first_shape = shaped((width, 3 * width), F32)
        second_shape = shaped((8, LANES), F32)
    accumulated = [
        shaped((8, width), F32),
        shaped((HEADS * TOKENS, LANES), F32),
        first_shape,
        second_shape,
    ]
    return launch(
        partial(back_kernel, per_step, carried is None, last_call),
        "attend_back",
        (count // per_step,),
        (where, normed, qkv, probs, grad_att, *fixed, *extra),
        [
            pl.BlockSpec(memory_space=pltpu.SMEM),
            row_spec(width),
            row_spec(3 * width),
            pl.BlockSpec((per_step // 2, HEADS * TOKENS, 2 * LANES), lambda i: (i + begin, 0, 0)),
            row_spec(width),
        ]
        + [whole(a.shape) for a in (*fixed, *extra)],
        [shaped(qkv.shape, BF16)] + accumulated,
        [row_spec(3 * width)] + [whole(a.shape) for a in accumulated],
        so_far=so_far,
        scratch=[
            pltpu.VMEM((width, 3 * width), F32),
            pltpu.VMEM((4, width, width), BF16),
        ],
        flops=count * TOKENS * width * width * 18,
        after=after,
        through=through,
        vmem=60,
    )


def images_kernel(first_call, where, grads, x_ref, grad_mid, gain, weight, *refs):
    carried = () if first_call else refs[:1]
    (gi_kept, gi_send, o_small, placed) = refs[len(carried) :]

    @pl.when(pl.program_id(0) == 0)
    def _():
        o_small[...] = jnp.zeros_like(o_small) if first_call else carried[0][...]

    product = dot_nt(grads[...], weight[...])
    gains = gain[...][None, :]
    sums = [jnp.zeros((8, product.shape[1]), F32)] * 2

    def rows_of(values, x, grad_middle):
        grad_normed = values.astype(BF16).astype(F32)
        hat, inverse = normalise(x.astype(F32))
        sums[0] = sums[0] + by_eights(grad_normed * hat)
        sums[1] = sums[1] + by_eights(grad_normed)
        return (grad_middle + normalise_back(grad_normed * gains, hat, inverse),)

    (grad_image,) = by_rows(rows_of, product, x_ref, grad_mid)
    o_small[0:1, :] += column_sum(sums[0])
    o_small[1:2, :] += column_sum(sums[1])
    placed[...] = grad_image.reshape(placed.shape)
    return_rows(where[0], placed, gi_kept, gi_send)


def image_grads(where, first, count, per_step, grads, x, grad_mid, gain, weight, shape, carried, so_far, after):
    total, _, cols, width = shape
    begin = first // per_step
    rows = per_step * TOKENS
    row_spec = lambda w: pl.BlockSpec((rows, w), lambda i: (i + begin, 0))
    fixed = (gain, weight, *carried)
    return launch(
        partial(images_kernel, not carried),
        "image_grads",
        (count // per_step,),
        (where, grads, x, grad_mid, *fixed),
        [pl.BlockSpec(memory_space=pltpu.SMEM), row_spec(3 * width), row_spec(width), row_spec(width)]
        + [whole(a.shape) for a in fixed],
        [
            shaped((total, GROUP, cols, width), F32),
            shaped((count, SENT, cols, width), BF16),
            shaped((8, width), F32),
        ],
        [
            pl.BlockSpec((per_step, GROUP, cols, width), lambda i: (i + begin, 0, 0, 0)),
            pl.BlockSpec((per_step, SENT, cols, width), lambda i: (i, 0, 0, 0)),
            whole((8, width)),
        ],
        so_far=so_far,
        scratch=[pltpu.VMEM((per_step, GROUP, PAD_COLS, width), F32)],
        flops=count * TOKENS * width * width * 6,
        after=after,
        vmem=32,
    )


def swap(value, flip):
    bands, batches = lax.axis_size("band"), lax.axis_size("batch")
    pairs = []
    for band in range(bands):
        for batch in range(batches):
            other = (band ^ flip[0]) * batches + (batch ^ flip[1])
            pairs.append((band * batches + batch, other))
    return lax.ppermute(value, ("band", "batch"), pairs)


def in_plane(value, d):
    return swap(value, (d >> 1, (d & 1) << 1))


PLANE = 4
ALONG = 4


def tree_sum(values):
    while len(values) > 1:
        values = [values[i] + values[i + 1] for i in range(0, len(values), 2)]
    return values[0]


def split_kernel(slot, count, small_rows, where, *refs):
    *refs, token = refs
    token[...] = jnp.zeros_like(token)
    outs = refs[-count - (1 if small_rows else 0) :]
    ins = refs[: len(refs) - len(outs)]
    me = where[slot]
    rows = outs[0].shape[0]
    if small_rows:
        ins, small_ins = ins[:small_rows], ins[small_rows:]
        small = tree_sum([r[...] if r.dtype == F32 else get_pair(r, r.shape[0] - 2 * SMALL) for r in small_ins])

    def total(index):
        start = pl.multiple_of(index * rows, rows)
        return tree_sum([ref[pl.ds(start, rows), :].astype(F32) for ref in ins])

    for d in range(count):
        outs[d][0:rows, :] = total(me ^ d).astype(outs[d].dtype)
        if small_rows and d > 0:
            put_pair(outs[d], rows, small)
    if small_rows:
        high = small.astype(BF16).astype(F32)
        outs[count][...] = high + (small - high).astype(BF16).astype(F32)


def split_share(where, slot, count, values, after, flops=0):
    rows, width = values[0].shape
    size = rows // count
    outs = [shaped((size, width), F32 if d == 0 else BF16) for d in range(count)] + [TOKEN]
    return small_launch(
        partial(split_kernel, slot, count, 0), "split_share", (where, *values), outs, after=after,
        flops=flops,
    )


def split_with_small(where, slot, count, values, smalls, after):
    rows, width = values[0].shape
    size = rows // count
    outs = [shaped((size, width), F32)] + [shaped((size + 2 * SMALL, width), BF16)] * (count - 1)
    outs += [shaped((SMALL, width), F32), TOKEN]
    return small_launch(
        partial(split_kernel, slot, count, len(values)), "split_with_small", (where, *values, *smalls), outs, after=after,
    )


def join_kernel(count, *refs):
    early, late = refs[:count], refs[count : 2 * count]
    small, share, small_out = refs[2 * count :]
    rows, more = early[0].shape[0], late[0].shape[0]
    share[0:rows, :] = tree_sum([r[...].astype(F32) for r in early]).astype(BF16)
    share[rows : rows + more, :] = tree_sum([r[0:more, :].astype(F32) for r in late]).astype(BF16)
    small_out[...] = tree_sum([small[...]] + [get_pair(r, more) for r in late[1:]])


def join_shares(early, late, small, after):
    rows, width = early[0].shape
    return small_launch(
        partial(join_kernel, len(early)),
        "join_shares",
        (*early, *late, small),
        [shaped((rows + late[0].shape[0], width), BF16), shaped((SMALL, width), F32)],
        after=after,
    )


def lay_kernel(slot, where, *refs):
    parts, (small, other, out, pair) = refs[:-4], refs[-4:]
    rows = parts[0].shape[0]
    for d, ref in enumerate(parts):
        out[pl.ds(pl.multiple_of((where[slot] ^ d) * rows, rows), rows), :] = ref[...]
    put_pair(pair, 0, small[...] + other[...])
    out[len(parts) * rows :, :] = pair[...]


def along(value, d):
    return swap(value, (0, 4 * d))


def spread(pieces, send):
    return [pieces[0]] + [send(piece, d) for d, piece in enumerate(pieces) if d > 0]


def gather_along(where, share, small, after):
    rows, width = share.shape
    parts = spread([share] * ALONG, along)
    return small_launch(
        partial(lay_kernel, 3),
        "lay",
        (where, *parts, small, swap(small, (0, 1))),
        [shaped((ALONG * rows + 2 * SMALL, width), BF16), shaped((2 * SMALL, width), BF16)],
        after=after,
    )


def halve_kernel(own, across, along_row, far, low, high, small):
    rows, cut = own.shape[0] - 2 * SMALL, low.shape[0]
    low[...] = across[0:cut, :]
    high[...] = along_row[cut:rows, :]
    small[...] = (get_pair(own, rows) + get_pair(along_row, rows)) + (get_pair(across, rows) + get_pair(far, 0))


def collect_kernel(across, along_row, low, high, out):
    rows, cut = out.shape[1], low.shape[0]
    out[0] = along_row[0:rows, :]
    out[1] = across[0:rows, :]
    out[2, 0:cut, :] = low[...]
    out[2, cut:rows, :] = high[...]


def gather_plane(quarter, pair, after, finish):
    theirs = swap(quarter, (0, 1))
    rows, width = quarter.shape[0] - 2 * SMALL, quarter.shape[1]
    across, along_row = in_plane(quarter, 2), in_plane(quarter, 1)
    cut = rows // 32 * 16
    low, high, small = small_launch(
        halve_kernel,
        "halve",
        (quarter, across, along_row, in_plane(pair, 3)),
        [shaped((cut, width), BF16), shaped((rows - cut, width), BF16), shaped((SMALL, width), F32)],
        after=after,
    )
    *smalls, token = finish(small)
    mine = small_launch(
        collect_kernel,
        "collect",
        (across, along_row, in_plane(low, 1), in_plane(high, 2)),
        [shaped((PLANE - 1, rows, width), BF16)],
        after=(token,),
    )[0]
    return smalls, (quarter, mine), (theirs, swap(mine, (0, 1)))


def unpack_kernel(flip, early, where, first, rest, o_w1, o_w2, o_qkv, o_proj, feed_buf, att_buf, sems):
    me, side = where[2], where[1] ^ flip
    width = o_proj.shape[0]
    late = width // 2 // ALONG
    low, high = slice(0, width // 2), slice(width // 2, width)
    def quarter_of(d):
        return first if d == 0 else rest.at[d - 1]

    def place(d):
        return pl.ds(pl.multiple_of((me ^ d) * width, width), width)

    for d in range(PLANE):
        for share in range(ALONG):
            start = share * (early + late) + early
            att_buf[me ^ d, share * late : (share + 1) * late, :] = quarter_of(d)[start : start + late, :].astype(F32)

    def run(att_targets, feed_target, turned):
        copies = []
        for index, (target, rows, cols) in enumerate(att_targets):
            copies.append(pltpu.make_async_copy(att_buf.at[index], target.at[rows, cols], sems.at[len(copies)]))
            copies[-1].start()
        for d in range(PLANE):
            shares = [quarter_of(d)[i * (early + late) : i * (early + late) + early, :] for i in range(ALONG)]
            block = jnp.concatenate(shares, axis=0).astype(F32)
            feed_buf[d] = block.T if turned else block
            copies.append(pltpu.make_async_copy(feed_buf.at[d], feed_target(d), sems.at[len(copies)]))
            copies[-1].start()
        for copy in copies:
            copy.wait()

    def halves(target, cols):
        return [(target, low, cols), (target, high, cols)]

    @pl.when(side == 0)
    def _():
        targets = halves(o_qkv, slice(0, width)) + halves(o_qkv, slice(width, 2 * width))
        run(targets, lambda d: o_w1.at[:, place(d)], False)

    @pl.when(side == 1)
    def _():
        targets = halves(o_qkv, slice(2 * width, 3 * width)) + halves(o_proj, slice(0, width))
        run(targets, lambda d: o_w2.at[place(d), :], True)


def unpack(flip, early, where, half, shapes, so_far):
    width = half[0].shape[1]
    vector = pl.BlockSpec(memory_space=pltpu.VMEM)
    return launch(
        partial(unpack_kernel, flip, early),
        "unpack",
        (),
        (where, *half),
        [pl.BlockSpec(memory_space=pltpu.SMEM), vector, vector],
        [shaped(shape, F32) for shape in shapes],
        [pl.BlockSpec(memory_space=pl.ANY)] * len(shapes),
        so_far=so_far,
        scratch=[
            pltpu.VMEM((PLANE, width, width), F32),
            pltpu.VMEM((PLANE, width // 2, width), F32),
            pltpu.SemaphoreType.DMA((2 * PLANE,)),
        ],
        vmem=24,
    )


def body(images, cotangent, norm1_gain, norm1_shift, qkv_weight, qv_bias, proj_weight, proj_bias, *rest):
    pos = rest[:13]
    norm2_gain, norm2_shift, fc1_weight, fc1_bias, fc2_weight, fc2_bias = rest[13:]
    total, _, cols, width = images.shape
    hidden = fc1_weight.shape[1]
    per_step = 4
    band, batch = lax.axis_index("band"), lax.axis_index("batch")
    where = jnp.stack([band, batch % 2, band * 2 + batch // 2 % 2, batch // 4 % ALONG]).astype(jnp.int32)
    head_of_row = np.arange(STACK)[:, None] // TOKENS
    mask = jnp.asarray(head_of_row == np.arange(LANES)[None, :] // HEAD_DIM, BF16)
    to_partner = lambda value: swap(value, (1, 0))
    pos = (*pos[:12], pos[12].T)

    later = (total // per_step * 2 // 5) * per_step
    image_chunks = [(0, later), (later, total - later)]
    packed, token = pack_rows((images,), [(0, *image_chunks[0])])
    received = to_partner(packed)
    later_packed, cot_packed, _ = pack_rows(
        (images, cotangent), [(0, *image_chunks[1]), (1, 0, total)], (token,)
    )
    pair, cot_packed = pair_bias(pos, (cot_packed,))
    later_received = to_partner(later_packed)
    norm_one = (norm1_gain, norm1_shift, qkv_weight, qv_bias, pair, mask)
    so_far = attend(where, images, received, 0, per_step, *norm_one, (), ())
    _, cot_packed = small_launch(
        token_kernel, "order", (), [TOKEN], after=(*so_far[:1], later_received), vmem=60, through=(cot_packed,)
    )
    cot_rows = to_partner(cot_packed)
    so_far = attend(where, images, later_received, later, per_step, *norm_one, so_far, ())
    x, normed, qkv, probs, att = so_far
    weights = (proj_weight, proj_bias, norm2_gain, norm2_shift, fc1_weight, fc1_bias, fc2_weight, fc2_bias)
    result = feed(where, cotangent, cot_rows, per_step, x, att, weights)
    out_images, grad_mid, grad_att, out_sent, feed_small, feed_b1, mine, theirs, grad_proj = result
    out_rows = to_partner(out_sent)
    flat = lambda value: value.reshape(-1, width)

    saved = (normed, qkv, probs, grad_att)
    chunks = [(0, total - later), (total - later, later)]
    theirs = swap(flat(theirs), (0, 1))
    *result, mine = attend_back(where, *chunks[0], per_step, saved, mask, grad_proj, None, (), False, (), (flat(mine),))
    early = [mine, theirs]
    *pieces, token = split_share(where, 2, PLANE, early, (out_rows,))
    early = spread(pieces, in_plane)
    result = attend_back(where, *chunks[1], per_step, saved, mask, grad_proj, result[1:4], result[:1], True,
                         (token,), ())
    grads, att_small, grad_pair = result[:3]
    mine, theirs = flat(result[3]), flat(result[4])
    *pieces, token = split_share(where, 3, ALONG, early, (att_small,), 5e9)
    early = spread(pieces, along)
    *pieces, token = split_share(where, 2, PLANE, [mine, swap(theirs, (0, 1))], (token,))
    late = spread(pieces, in_plane)
    grad_images, sent, norm_small = image_grads(where, 0, total, per_step, grads, x, grad_mid, norm1_gain,
                                                qkv_weight, images.shape, (), (), (token,))
    grad_rows = to_partner(sent)
    small = gather_small(feed_small, feed_b1, att_small, norm_small, grad_pair)
    *pieces, small, _ = split_with_small(where, 3, ALONG, late, [small], early[1:])
    late = spread(pieces, along)
    share, small = join_shares(early, late, small, ())
    stride = PLANE * ALONG
    while stride < lax.axis_size("batch"):
        share = (share.astype(F32) + swap(share, (0, stride)).astype(F32)).astype(BF16)
        small = small + swap(small, (0, stride))
        stride *= 2
    out_images, token = merge_rows(out_rows, out_images, 0)
    quarter, own_pair = gather_along(where, share, small, (token,))
    grad_images, token = merge_rows(grad_rows, grad_images, 0)
    smalls, half, other_half = gather_plane(
        quarter, own_pair, (token,), lambda small: finish_small(pos, small, hidden)
    )
    shapes = [w.shape for w in (fc1_weight, fc2_weight, qkv_weight, proj_weight)]
    large = unpack(0, early[0].shape[0], where, half, shapes, ())
    grad_fc1, grad_fc2, grad_qkv, grad_proj = unpack(1, early[0].shape[0], where, other_half, shapes, large)
    n1_gain, n1_shift, qv, proj_b, n2_gain, n2_shift, fc1_b, fc2_b = smalls[:8]
    return (out_images, grad_images, n1_gain, n1_shift, grad_qkv, qv, grad_proj, proj_b, *smalls[8:20], smalls[20].T,
            n2_gain, n2_shift, grad_fc1, fc1_b, grad_fc2, fc2_b)


def solution(mesh):
    tokens = P("batch", "band", None, None)
    return jax.shard_map(
        body,
        mesh=mesh,
        in_specs=(tokens, tokens) + (P(),) * 25,
        out_specs=(tokens, tokens) + (P(),) * 25,
        check_vma=False,
    )
```

```python
import math
from functools import partial

import jax
import jax.numpy as jnp
import numpy as np
from jax import lax
from jax.experimental import pallas as pl
from jax.experimental.pallas import tpu as pltpu
from jax.sharding import PartitionSpec as P

HEADS = 12
GROUP = 7
HEAD_DIM = 32
SPAN = 2 * GROUP - 1
HIGH = lax.Precision.HIGHEST
EPSILON = 1e-05
SCALE = HEAD_DIM**-0.5
MASKED = -1e30
PAD_COLS = 16
TOKENS = GROUP * PAD_COLS
LANES = 128
PER_BLOCK = LANES // HEAD_DIM
STACK = PER_BLOCK * TOKENS
KEPT = (GROUP + 1) // 2
SENT = GROUP - KEPT
OFFSETS = 176
WIDE = SPAN * PAD_COLS
F32 = jnp.float32
BF16 = jnp.bfloat16


def dot(a, b, precision=None):
    return lax.dot_general(a, b, (((1,), (0,)), ((), ())), precision=precision, preferred_element_type=F32)


def dot_nt(a, b, precision=None):
    return lax.dot_general(a, b, (((1,), (1,)), ((), ())), precision=precision, preferred_element_type=F32)


def dot_tn(a, b, precision=None):
    return lax.dot_general(a, b, (((0,), (0,)), ((), ())), precision=precision, preferred_element_type=F32)


def whole(shape):
    zeros = (0,) * len(shape)
    return pl.BlockSpec(shape, lambda *_: zeros, pipeline_mode=pl.Buffered(1))


def normalise(values):
    mean = jnp.mean(values, axis=-1, keepdims=True)
    centred = values - mean
    inverse = lax.rsqrt(jnp.mean(centred * centred, axis=-1, keepdims=True) + EPSILON)
    return centred * inverse, inverse


def normalise_back(grad_hat, hat, inverse):
    first = jnp.mean(grad_hat, axis=-1, keepdims=True)
    second = jnp.mean(grad_hat * hat, axis=-1, keepdims=True)
    return inverse * (grad_hat - first - hat * second)


def gelu_both(v):
    cdf = 0.5 + 0.5 * lax.erf(v * (0.5**0.5))
    density = jnp.exp(-0.5 * v * v) * ((2.0 * np.pi) ** -0.5)
    return v * cdf, cdf + v * density


def column_sum(values):
    return jnp.sum(values, axis=0, keepdims=True)


SMALL = 24


def launch(kernel, name, grid, inputs, in_specs, out_shape, out_specs, so_far=(), scratch=(), flops=0,
           after=(), vmem=16, through=()):
    count, held = len(inputs), len(so_far) + len(after) + len(through)
    own = len(out_shape)
    hand = {count + len(so_far) + len(after) + i: own + i for i in range(len(through))}
    inner = kernel
    if held:
        kernel = lambda *refs: inner(
            *refs[:count], *refs[count + held : count + held + own], *refs[count + held + own + len(through) :]
        )
    moved = sum(a.size * a.dtype.itemsize for a in (*inputs, *out_shape))
    return pl.pallas_call(
        kernel,
        grid=grid,
        in_specs=list(in_specs) + [pl.BlockSpec(memory_space=pl.ANY)] * held,
        out_specs=list(out_specs) + [pl.BlockSpec(memory_space=pl.ANY)] * len(through),
        out_shape=list(out_shape) + [shaped(a.shape, a.dtype) for a in through],
        input_output_aliases={count + i: i for i in range(len(so_far))} | hand,
        scratch_shapes=list(scratch),
        compiler_params=pltpu.CompilerParams(vmem_limit_bytes=vmem * 2**20),
        cost_estimate=pl.CostEstimate(flops=int(flops), bytes_accessed=int(moved), transcendentals=0),
        name=name,
    )(*inputs, *so_far, *after, *through)


def small_launch(kernel, name, inputs, out_shape, scratch=(), flops=0, after=(), vmem=16, through=()):
    specs = [pl.BlockSpec(memory_space=pltpu.SMEM if a.dtype == jnp.int32 else pltpu.VMEM) for a in inputs]
    outs = [pl.BlockSpec(memory_space=pltpu.VMEM)] * len(out_shape)
    return launch(kernel, name, (), inputs, specs, out_shape, outs, scratch=scratch, flops=flops, after=after, vmem=vmem,
                  through=through)


def shaped(shape, dtype):
    return jax.ShapeDtypeStruct(shape, dtype)


FEED_PART = 512
TOKEN = shaped((8, LANES), F32)


def token_kernel(token):
    token[...] = jnp.zeros_like(token)


def merge_kernel(source, target, token):
    target[...] = source[...].astype(target.dtype)
    token[...] = jnp.zeros_like(token)


def pack_kernel(pieces, *refs):
    count = 1 + max(piece[0] for piece in pieces)
    sources, outs, (token, sems) = refs[:count], refs[count:-2], refs[-2:]
    token[...] = jnp.zeros_like(token)
    copies = []
    for (source, first, images), out in zip(pieces, outs):
        for row in range(SENT):
            copies.append(
                pltpu.make_async_copy(
                    sources[source].at[first : first + images, 2 * row + 1], out.at[:, row], sems.at[len(copies)]
                )
            )
    for copy in copies:
        copy.start()
    for copy in copies:
        copy.wait()


def pack_rows(sources, pieces, after=()):
    _, _, cols, width = sources[0].shape
    vector = pl.BlockSpec(memory_space=pltpu.VMEM)
    return launch(
        partial(pack_kernel, pieces),
        "pack_rows",
        (),
        sources,
        [pl.BlockSpec(memory_space=pl.ANY)] * len(sources),
        [shaped((count, SENT, cols, width), BF16) for _, _, count in pieces] + [TOKEN],
        [vector] * (len(pieces) + 1),
        scratch=[pltpu.SemaphoreType.DMA((SENT * len(pieces),))],
        after=after,
        vmem=60,
    )


def merge_rows(received, target, first):
    count, _, cols, width = received.shape
    unit = math.gcd(first, count)
    begin = first // unit
    return launch(
        merge_kernel,
        "merge_rows",
        (count // unit, SENT),
        (received,),
        [pl.BlockSpec((unit, 1, cols, width), lambda i, r: (i, r, 0, 0))],
        [shaped(target.shape, target.dtype), TOKEN],
        [pl.BlockSpec((unit, 1, cols, width), lambda i, r: (i + begin, 2 * r + 1, 0, 0)), whole(TOKEN.shape)],
        so_far=(target,),
    )


def position_layers(refs):
    (in_w, in_b, g1, s1, w1, b1, g2, s2, w2, b2, g3, s3, _) = refs
    width = in_w.shape[1]
    offset = lax.broadcasted_iota(jnp.int32, (OFFSETS, width), 0)
    rows = (offset // SPAN - (GROUP - 1)).astype(F32)
    cols = (offset % SPAN - (GROUP - 1)).astype(F32)
    hidden = rows * in_w[0:1, :] + cols * in_w[1:2, :] + in_b[...][None, :]
    kept = []
    for gain, shift, weight, bias in ((g1, s1, w1, b1), (g2, s2, w2, b2), (g3, s3, None, None)):
        hat, inverse = normalise(hidden)
        active, slope = gelu_both(hat * gain[...][None, :] + shift[...][None, :])
        kept.append((hat, inverse, active, slope))
        if weight is not None:
            hidden = dot(active, weight[...], HIGH) + bias[...][None, :]
    return rows, cols, kept


def pick_offsets(place):
    offset = lax.broadcasted_iota(jnp.int32, (OFFSETS, WIDE), 0)
    lane = lax.broadcasted_iota(jnp.int32, (OFFSETS, WIDE), 1)
    wanted = lane // PAD_COLS * SPAN + lane % PAD_COLS // 2 - place + GROUP - 1
    return jnp.where(offset == wanted, 1.0, 0.0).astype(F32)


def bias_kernel(*refs):
    ins, (out, strip) = refs[:13], refs[13:]
    _, _, kept = position_layers(ins)
    table = dot_nt(ins[12][...], kept[2][2], HIGH)
    lane = lax.broadcasted_iota(jnp.int32, (HEADS, WIDE), 1)
    even = lane % 2 == 0
    strip[...] = jnp.full(strip.shape, MASKED, F32)
    for place in range(GROUP):
        spread = dot(table, pick_offsets(place), HIGH)
        strip[:, 2 * place, 0:WIDE] = jnp.where(even, spread, MASKED)
        strip[:, 2 * place + 1, 0:WIDE] = jnp.where(even, MASKED, spread)
    out[...] = jnp.zeros_like(out)
    for row in range(GROUP):
        start = (GROUP - 1 - row) * PAD_COLS
        out[:, row * PAD_COLS : (row + 1) * PAD_COLS, 0:TOKENS] = strip[:, :, start : start + TOKENS]


def pair_bias(pos, through):
    return small_launch(
        bias_kernel,
        "pair_bias",
        pos,
        [shaped((HEADS, TOKENS, LANES), F32)],
        [pltpu.VMEM((HEADS, PAD_COLS, 2 * LANES), F32)],
        through=through,
        vmem=60,
    )


def put_pair(ref, start, values):
    high = values.astype(BF16)
    ref[start : start + SMALL, :] = high
    ref[start + SMALL : start + 2 * SMALL, :] = (values - high.astype(F32)).astype(BF16)


def get_pair(ref, start):
    return ref[start : start + SMALL, :].astype(F32) + ref[start + SMALL : start + 2 * SMALL, :].astype(F32)


def gather_small_kernel(feed_small, feed_b1, att_small, norm_small, grad_pair, out, small):
    width = feed_small.shape[1]
    strip = jnp.zeros((HEADS, PAD_COLS, WIDE), F32)
    for row in range(GROUP):
        start = (GROUP - 1 - row) * PAD_COLS
        piece = grad_pair[:, row * PAD_COLS : (row + 1) * PAD_COLS, 0:TOKENS]
        strip = strip + jnp.pad(piece, ((0, 0), (0, 0), (start, WIDE - start - TOKENS)))
    table = jnp.zeros((HEADS, OFFSETS), F32)
    for place in range(GROUP):
        folded = strip[:, 2 * place, :] + strip[:, 2 * place + 1, :]
        table = table + dot_nt(folded, pick_offsets(place), HIGH)
    small[...] = jnp.zeros_like(small)
    small[0:4, :] = feed_small[0:4, :]
    small[4:6, :] = norm_small[0:2, :]
    small[6:8, :] = att_small[0:2, :]
    for part in range(feed_b1.shape[1] // width):
        small[8 + part : 9 + part, :] = feed_b1[:, part * width : (part + 1) * width]
    small[12 : 12 + HEADS, 0:OFFSETS] = table
    put_pair(out, 0, small[...])


def gather_small(feed_small, feed_b1, att_small, norm_small, grad_pair):
    width = feed_small.shape[1]
    return small_launch(
        gather_small_kernel,
        "gather_small",
        (feed_small, feed_b1, att_small, norm_small, grad_pair.reshape(HEADS, TOKENS, LANES)),
        [shaped((2 * SMALL, width), BF16)],
        [pltpu.VMEM((SMALL, width), F32)],
    )[0]


def finish_small_kernel(*refs):
    ins, small, outs = refs[:13], refs[13], refs[14:]
    (in_w, in_b, g1, s1, w1, b1, g2, s2, w2, b2, g3, s3, w3) = ins
    (o_n1_gain, o_n1_shift, o_qv, o_proj_b, o_n2_gain, o_n2_shift, o_fc1_b, o_fc2_b) = outs[:8]
    (o_in_w, o_in_b, o_g1, o_s1, o_w1, o_b1, o_g2, o_s2, o_w2, o_b2, o_g3, o_s3, o_w3) = outs[8:]
    o_n2_gain[...] = small[0, :]
    o_n2_shift[...] = small[1, :]
    o_fc2_b[...] = small[2, :]
    o_proj_b[...] = small[3, :]
    o_n1_gain[...] = small[4, :]
    o_n1_shift[...] = small[5, :]
    o_qv[...] = small[6:8, :]
    width = small.shape[1]
    for part in range(o_fc1_b.shape[0] // width):
        o_fc1_b[part * width : (part + 1) * width] = small[8 + part, :]
    rows, cols, kept = position_layers(ins)
    table = small[12 : 12 + HEADS, 0:OFFSETS]
    o_w3[...] = dot(table, kept[2][2], HIGH)
    grad_active = dot(table.T, w3[...], HIGH)
    stages = (
        (g3, o_g3, o_s3, o_b2, o_w2, w2),
        (g2, o_g2, o_s2, o_b1, o_w1, w1),
        (g1, o_g1, o_s1, o_in_b, None, None),
    )
    for level, (gain, o_gain, o_shift, o_bias, o_weight, weight) in zip((2, 1, 0), stages):
        hat, inverse, _, slope = kept[level]
        grad_norm = grad_active * slope
        o_gain[...] = jnp.sum(grad_norm * hat, axis=0)
        o_shift[...] = jnp.sum(grad_norm, axis=0)
        grad_hidden = normalise_back(grad_norm * gain[...][None, :], hat, inverse)
        o_bias[...] = jnp.sum(grad_hidden, axis=0)
        if weight is not None:
            o_weight[...] = dot(kept[level - 1][2].T, grad_hidden, HIGH)
            grad_active = dot_nt(grad_hidden, weight[...], HIGH)
        else:
            o_in_w[0:1, :] = column_sum(grad_hidden * rows)
            o_in_w[1:2, :] = column_sum(grad_hidden * cols)


def finish_small(pos, small, hidden):
    width = small.shape[1]
    shapes = [(width,), (width,), (2, width), (width,), (width,), (width,), (hidden,), (width,)]
    return small_launch(
        finish_small_kernel,
        "finish_small",
        (*pos, small),
        [shaped(s, F32) for s in shapes] + [shaped(p.shape, F32) for p in pos],
    )


def stack_heads(block, mask):
    return jnp.concatenate([block] * PER_BLOCK, axis=0) * mask


def two_images(two):
    return [slice(image * TOKENS, (image + 1) * TOKENS) for image in (2 * two, 2 * two + 1)]


def on_diagonal(blocks):
    rest = jnp.zeros((LANES - TOKENS, LANES), BF16)
    zero = jnp.zeros((LANES, LANES), BF16)
    first, second = [jnp.concatenate([block, rest], axis=0) for block in blocks]
    return jnp.concatenate(
        [jnp.concatenate([first, zero], axis=1), jnp.concatenate([zero, second], axis=1)], axis=0
    )


def side_by_side(blocks, mask):
    return jnp.concatenate([stack_heads(block, mask) for block in blocks], axis=1)


def place_rows(band, kept_ref, received_ref, padded):
    upper = band * SENT
    lower = (1 - band) * KEPT
    for row in range(KEPT):
        padded[:, row + upper, 0 : 2 * GROUP, :] = kept_ref[:, 2 * row]
    for row in range(SENT):
        padded[:, row + lower, 0 : 2 * GROUP, :] = received_ref[:, row]


def return_rows(band, placed, kept_ref, sent_ref):
    upper = band * SENT
    lower = (1 - band) * KEPT
    for row in range(KEPT):
        kept_ref[:, 2 * row] = placed[:, row + upper, 0 : 2 * GROUP, :]
    for row in range(SENT):
        sent_ref[:, row] = placed[:, row + lower, 0 : 2 * GROUP, :].astype(sent_ref.dtype)


def attend_kernel(count, where, images, received, gain, shift, weight, bias, pair, mask,
                  x_out, normed_out, qkv_out, probs_out, att_out, padded):
    width = images.shape[3]

    @pl.when(pl.program_id(0) == 0)
    def _():
        padded[...] = jnp.zeros_like(padded)

    place_rows(where[0], images, received, padded)
    x = padded[...].reshape(count * TOKENS, width)
    x_out[...] = x
    hat, _ = normalise(x.astype(F32))
    normed = (hat * gain[...][None, :] + shift[...][None, :]).astype(BF16)
    normed_out[...] = normed
    piece = dot(normed, weight[...])
    qkv_out[:, 0:width] = (piece[:, 0:width] + bias[0:1, :]).astype(BF16)
    qkv_out[:, width : 2 * width] = piece[:, width : 2 * width].astype(BF16)
    qkv_out[:, 2 * width :] = (piece[:, 2 * width :] + bias[1:2, :]).astype(BF16)
    masks = mask[...]
    for two in range(count // 2):
        both = two_images(two)
        for block in range(HEADS // PER_BLOCK):
            at = block * LANES
            here = slice(block * STACK, (block + 1) * STACK)
            query = on_diagonal([qkv_out[rows, at : at + LANES] for rows in both])
            keys = side_by_side([qkv_out[rows, width + at : width + at + LANES] for rows in both], masks)
            scores = dot_nt(keys, query) * SCALE + jnp.concatenate([pair[here, :]] * 2, axis=1)
            scores = scores.reshape(PER_BLOCK, TOKENS, 2 * LANES)
            probs = jnp.exp(scores - jnp.max(scores, axis=1, keepdims=True))
            probs = probs * (1.0 / jnp.sum(probs, axis=1, keepdims=True))
            probs = probs.astype(BF16).reshape(STACK, 2 * LANES)
            probs_out[two, here, :] = probs
            for half, rows in enumerate(both):
                vals = stack_heads(qkv_out[rows, 2 * width + at : 2 * width + at + LANES], masks)
                attended = dot_tn(probs[:, half * LANES : (half + 1) * LANES], vals)
                att_out[rows, at : at + LANES] = attended[0:TOKENS, :].astype(BF16)


def attend(where, images, received, first, per_step, gain, shift, weight, bias, pair, mask, so_far, through):
    total, _, cols, width = images.shape
    count = received.shape[0]
    begin = first // per_step
    rows = per_step * TOKENS
    row_spec = lambda w: pl.BlockSpec((rows, w), lambda i: (i + begin, 0))
    fixed = (gain, shift, weight, bias, pair.reshape(HEADS * TOKENS, LANES), mask)
    return launch(
        partial(attend_kernel, per_step),
        "attend",
        (count // per_step,),
        (where, images, received, *fixed),
        [
            pl.BlockSpec(memory_space=pltpu.SMEM),
            pl.BlockSpec((per_step, GROUP, cols, width), lambda i: (i + begin, 0, 0, 0)),
            pl.BlockSpec((per_step, SENT, cols, width), lambda i: (i, 0, 0, 0)),
        ]
        + [whole(a.shape) for a in fixed],
        [
            shaped((total * TOKENS, width), BF16),
            shaped((total * TOKENS, width), BF16),
            shaped((total * TOKENS, 3 * width), BF16),
            shaped((total // 2, HEADS * TOKENS, 2 * LANES), BF16),
            shaped((total * TOKENS, width), BF16),
        ],
        [
            row_spec(width),
            row_spec(width),
            row_spec(3 * width),
            pl.BlockSpec((per_step // 2, HEADS * TOKENS, 2 * LANES), lambda i: (i + begin, 0, 0)),
            row_spec(width),
        ],
        so_far=so_far,
        scratch=[pltpu.VMEM((per_step, GROUP, PAD_COLS, width), BF16)],
        flops=count * TOKENS * width * width * 12,
        through=through,
        vmem=60,
    )


def feed_kernel(count, where, cot, received, x_ref, att_ref, proj_w, proj_b, gain, shift, w1, b1, w2, b2,
                out_kept, grad_mid, grad_att, out_send, o_small, o_b1, o_first, o_second, a_proj,
                padded, placed, pair):
    width = x_ref.shape[1]
    hidden = w1.shape[1]
    step = pl.program_id(0)

    @pl.when(step == 0)
    def _():
        for ref in (padded, o_small, o_b1, pair, a_proj):
            ref[...] = jnp.zeros_like(ref)

    place_rows(where[0], cot, received, padded)
    up = padded[...].reshape(count * TOKENS, width)
    up_f = up.astype(F32)
    up_turned = up.T
    att = att_ref[...]
    middle = x_ref[...].astype(F32) + (dot(att, proj_w[...]) + proj_b[...][None, :])
    hat, inverse = normalise(middle)
    normed = (hat * gain[...][None, :] + shift[...][None, :]).astype(BF16)
    normed_turned = normed.T
    result = middle + b2[...][None, :]
    grad_normed = jnp.zeros((count * TOKENS, width), F32)
    starts = range(0, hidden, FEED_PART)

    def ahead(start):
        cols = slice(start, start + FEED_PART)
        return dot(normed, w1[:, cols]), dot_nt(up, w2[cols, :])

    coming = ahead(0)
    for start in starts:
        cols = slice(start, start + FEED_PART)
        pre_act, grad_act = coming
        if start + FEED_PART < hidden:
            coming = ahead(start + FEED_PART)
        active, slope = gelu_both(pre_act + b1[cols][None, :])
        active = active.astype(BF16)
        grad_pre = grad_act * slope
        o_b1[:, cols] += column_sum(grad_pre)
        grad_pre = grad_pre.astype(BF16)
        result = result + dot(active, w2[cols, :])
        grad_normed = grad_normed + dot_nt(grad_pre, w1[:, cols])
        pair[0, :, cols] += dot(normed_turned, grad_pre)
        pair[1, :, cols] += dot(up_turned, active)
    placed[...] = result.astype(BF16).reshape(placed.shape)
    return_rows(where[0], placed, out_kept, out_send)
    grad_normed = grad_normed.astype(BF16).astype(F32)
    grad_middle = up_f + normalise_back(grad_normed * gain[...][None, :], hat, inverse)
    grad_mid[...] = grad_middle
    branch = grad_middle.astype(BF16)
    a_proj[...] += dot(att.T, branch)
    grad_att[...] = dot_nt(branch, proj_w[...]).astype(BF16)
    o_small[0:1, :] += column_sum(grad_normed * hat)
    o_small[1:2, :] += column_sum(grad_normed)
    o_small[2:3, :] += column_sum(up_f)
    o_small[3:4, :] += column_sum(branch.astype(F32))

    @pl.when(step == pl.num_programs(0) - 1)
    def _():
        core = where[1]
        for part in range(hidden // width):
            cols = slice(part * width, (part + 1) * width)
            o_first[part] = pair[core, :, cols].astype(BF16)
            o_second[part] = pair[1 - core, :, cols].astype(BF16)


def feed(where, cotangent, received, per_step, x, att, weights):
    total, _, cols, width = cotangent.shape
    hidden = weights[4].shape[1]
    rows = per_step * TOKENS
    row_spec = lambda w: pl.BlockSpec((rows, w), lambda i: (i, 0))
    image_spec = lambda n: pl.BlockSpec((per_step, n, cols, width), lambda i: (i, 0, 0, 0))
    accumulated = [
        shaped((8, width), F32),
        shaped((1, hidden), F32),
        shaped((hidden // width, width, width), BF16),
        shaped((hidden // width, width, width), BF16),
        shaped((width, width), F32),
    ]
    return launch(
        partial(feed_kernel, per_step),
        "feed",
        (total // per_step,),
        (where, cotangent, received, x, att, *weights),
        [pl.BlockSpec(memory_space=pltpu.SMEM), image_spec(GROUP), image_spec(SENT), row_spec(width), row_spec(width)]
        + [whole(a.shape) for a in weights],
        [
            shaped((total, GROUP, cols, width), BF16),
            shaped((total * TOKENS, width), F32),
            shaped((total * TOKENS, width), BF16),
            shaped((total, SENT, cols, width), BF16),
        ]
        + accumulated,
        [image_spec(GROUP), row_spec(width), row_spec(width), image_spec(SENT)]
        + [whole(a.shape) for a in accumulated],
        scratch=[
            pltpu.VMEM((per_step, GROUP, PAD_COLS, width), BF16),
            pltpu.VMEM((per_step, GROUP, PAD_COLS, width), BF16),
            pltpu.VMEM((2, width, hidden), F32),
        ],
        flops=total * TOKENS * width * width * 54,
        vmem=60,
    )


def pick_heads(stacked):
    parts = stacked.reshape(PER_BLOCK, TOKENS, LANES)
    lane = lax.broadcasted_iota(jnp.int32, (TOKENS, LANES), 1)
    picked = parts[PER_BLOCK - 1]
    for head in range(PER_BLOCK - 2, -1, -1):
        picked = jnp.where(lane < (head + 1) * HEAD_DIM, parts[head], picked)
    return picked


def back_kernel(count, first_call, last_call, where, normed, qkv, probs_ref, grad_att, mask, a_proj, *refs):
    carried = () if first_call else refs[:3]
    (grads, o_small, o_pair, o_first, o_second, a_w, packed) = refs[len(carried) :]
    width = normed.shape[1]
    step = pl.program_id(0)

    @pl.when(step == 0)
    def _():
        for index, ref in enumerate((o_small, o_pair, a_w)):
            ref[...] = jnp.zeros_like(ref) if first_call else carried[index][...]

    masks = mask[...]
    for two in range(count // 2):
        both = two_images(two)
        for block in range(HEADS // PER_BLOCK):
            at = block * LANES
            here = slice(block * STACK, (block + 1) * STACK)
            query = on_diagonal([qkv[rows, at : at + LANES] for rows in both])
            grad = on_diagonal([grad_att[rows, at : at + LANES] for rows in both])
            vals = side_by_side([qkv[rows, 2 * width + at : 2 * width + at + LANES] for rows in both], masks)
            probs = probs_ref[two, here, :]
            exact = probs.astype(F32).reshape(PER_BLOCK, TOKENS, 2 * LANES)
            grad_probs = dot_nt(vals, grad).reshape(PER_BLOCK, TOKENS, 2 * LANES)
            inner = jnp.sum(grad_probs * exact, axis=1, keepdims=True)
            exact_scores = (exact * (grad_probs - inner)).reshape(STACK, 2 * LANES)
            o_pair[here, :] += exact_scores[:, :LANES] + exact_scores[:, LANES:]
            grad_scores = exact_scores.astype(BF16)
            grad_keys = dot(grad_scores, query)
            grad_vals = dot(probs, grad)
            for half, rows in enumerate(both):
                lanes = slice(half * LANES, (half + 1) * LANES)
                keys = stack_heads(qkv[rows, width + at : width + at + LANES], masks)
                grad_query = dot_tn(grad_scores[:, lanes], keys)[0:TOKENS, :]
                grads[rows, at : at + LANES] = (grad_query * SCALE).astype(BF16)
                grads[rows, width + at : width + at + LANES] = (
                    pick_heads(grad_keys[:, lanes]) * SCALE
                ).astype(BF16)
                grads[rows, 2 * width + at : 2 * width + at + LANES] = pick_heads(grad_vals[:, lanes]).astype(BF16)
    all_grads = grads[...]
    a_w[...] += dot(normed[...].T, all_grads)
    o_small[0:1, :] += column_sum(all_grads[:, :width].astype(F32))
    o_small[1:2, :] += column_sum(all_grads[:, 2 * width :].astype(F32))

    @pl.when(step == pl.num_programs(0) - 1)
    def _():
        if last_call:
            core = where[1]
            for part in range(3):
                packed[part] = a_w[:, part * width : (part + 1) * width].astype(BF16)
            packed[3] = a_proj[...].astype(BF16)
            for part in range(2):
                o_first[part] = packed[2 * core + part]
                o_second[part] = packed[2 - 2 * core + part]
        else:
            o_first[...] = a_w[...]
            o_second[...] = jnp.zeros_like(o_second)


def attend_back(where, first, count, per_step, saved, mask, grad_proj, carried, so_far, last_call, after):
    normed, qkv, probs, grad_att = saved
    width = normed.shape[1]
    begin = first // per_step
    rows = per_step * TOKENS
    extra = () if carried is None else tuple(carried)
    row_spec = lambda w: pl.BlockSpec((rows, w), lambda i: (i + begin, 0))
    fixed = (mask, grad_proj)
    if last_call:
        first_shape = second_shape = shaped((2, width, width), BF16)
    else:
        first_shape = shaped((width, 3 * width), F32)
        second_shape = shaped((8, LANES), F32)
    accumulated = [
        shaped((8, width), F32),
        shaped((HEADS * TOKENS, LANES), F32),
        first_shape,
        second_shape,
    ]
    return launch(
        partial(back_kernel, per_step, carried is None, last_call),
        "attend_back",
        (count // per_step,),
        (where, normed, qkv, probs, grad_att, *fixed, *extra),
        [
            pl.BlockSpec(memory_space=pltpu.SMEM),
            row_spec(width),
            row_spec(3 * width),
            pl.BlockSpec((per_step // 2, HEADS * TOKENS, 2 * LANES), lambda i: (i + begin, 0, 0)),
            row_spec(width),
        ]
        + [whole(a.shape) for a in (*fixed, *extra)],
        [shaped(qkv.shape, BF16)] + accumulated,
        [row_spec(3 * width)] + [whole(a.shape) for a in accumulated],
        so_far=so_far,
        scratch=[
            pltpu.VMEM((width, 3 * width), F32),
            pltpu.VMEM((4, width, width), BF16),
        ],
        flops=count * TOKENS * width * width * 18,
        after=after,
        vmem=60,
    )


def images_kernel(first_call, where, grads, x_ref, grad_mid, gain, weight, *refs):
    carried = () if first_call else refs[:1]
    (gi_kept, gi_send, o_small, placed) = refs[len(carried) :]

    @pl.when(pl.program_id(0) == 0)
    def _():
        o_small[...] = jnp.zeros_like(o_small) if first_call else carried[0][...]

    grad_normed = dot_nt(grads[...], weight[...]).astype(BF16).astype(F32)
    hat, inverse = normalise(x_ref[...].astype(F32))
    o_small[0:1, :] += column_sum(grad_normed * hat)
    o_small[1:2, :] += column_sum(grad_normed)
    grad_image = grad_mid[...] + normalise_back(grad_normed * gain[...][None, :], hat, inverse)
    placed[...] = grad_image.reshape(placed.shape)
    return_rows(where[0], placed, gi_kept, gi_send)


def image_grads(where, first, count, per_step, grads, x, grad_mid, gain, weight, shape, carried, so_far, after):
    total, _, cols, width = shape
    begin = first // per_step
    rows = per_step * TOKENS
    row_spec = lambda w: pl.BlockSpec((rows, w), lambda i: (i + begin, 0))
    fixed = (gain, weight, *carried)
    return launch(
        partial(images_kernel, not carried),
        "image_grads",
        (count // per_step,),
        (where, grads, x, grad_mid, *fixed),
        [pl.BlockSpec(memory_space=pltpu.SMEM), row_spec(3 * width), row_spec(width), row_spec(width)]
        + [whole(a.shape) for a in fixed],
        [
            shaped((total, GROUP, cols, width), F32),
            shaped((count, SENT, cols, width), BF16),
            shaped((8, width), F32),
        ],
        [
            pl.BlockSpec((per_step, GROUP, cols, width), lambda i: (i + begin, 0, 0, 0)),
            pl.BlockSpec((per_step, SENT, cols, width), lambda i: (i, 0, 0, 0)),
            whole((8, width)),
        ],
        so_far=so_far,
        scratch=[pltpu.VMEM((per_step, GROUP, PAD_COLS, width), F32)],
        flops=count * TOKENS * width * width * 6,
        after=after,
        vmem=32,
    )


def swap(value, flip):
    bands, batches = lax.axis_size("band"), lax.axis_size("batch")
    pairs = []
    for band in range(bands):
        for batch in range(batches):
            other = (band ^ flip[0]) * batches + (batch ^ flip[1])
            pairs.append((band * batches + batch, other))
    return lax.ppermute(value, ("band", "batch"), pairs)


def in_plane(value, d):
    return swap(value, (d >> 1, (d & 1) << 1))


PLANE = 4
ALONG = 4


def tree_sum(values):
    while len(values) > 1:
        values = [values[i] + values[i + 1] for i in range(0, len(values), 2)]
    return values[0]


def split_kernel(slot, count, small_rows, where, *refs):
    *refs, token = refs
    token[...] = jnp.zeros_like(token)
    outs = refs[-count - (1 if small_rows else 0) :]
    ins = refs[: len(refs) - len(outs)]
    me = where[slot]
    rows = outs[0].shape[0]
    if small_rows:
        ins, small_ins = ins[:small_rows], ins[small_rows:]
        small = tree_sum([r[...] if r.dtype == F32 else get_pair(r, r.shape[0] - 2 * SMALL) for r in small_ins])

    def total(index):
        start = pl.multiple_of(index * rows, rows)
        return tree_sum([ref[pl.ds(start, rows), :].astype(F32) for ref in ins])

    for d in range(count):
        outs[d][0:rows, :] = total(me ^ d).astype(outs[d].dtype)
        if small_rows and d > 0:
            put_pair(outs[d], rows, small)
    if small_rows:
        high = small.astype(BF16).astype(F32)
        outs[count][...] = high + (small - high).astype(BF16).astype(F32)


def split_share(where, slot, count, values, after, flops=0):
    rows, width = values[0].shape
    size = rows // count
    outs = [shaped((size, width), F32 if d == 0 else BF16) for d in range(count)] + [TOKEN]
    return small_launch(
        partial(split_kernel, slot, count, 0), "split_share", (where, *values), outs, after=after,
        flops=flops,
    )


def split_with_small(where, slot, count, values, smalls, after):
    rows, width = values[0].shape
    size = rows // count
    outs = [shaped((size, width), F32)] + [shaped((size + 2 * SMALL, width), BF16)] * (count - 1)
    outs += [shaped((SMALL, width), F32), TOKEN]
    return small_launch(
        partial(split_kernel, slot, count, len(values)), "split_with_small", (where, *values, *smalls), outs, after=after,
    )


def join_kernel(count, *refs):
    early, late = refs[:count], refs[count : 2 * count]
    small, share, small_out = refs[2 * count :]
    rows, more = early[0].shape[0], late[0].shape[0]
    share[0:rows, :] = tree_sum([r[...].astype(F32) for r in early]).astype(BF16)
    share[rows : rows + more, :] = tree_sum([r[0:more, :].astype(F32) for r in late]).astype(BF16)
    small_out[...] = tree_sum([small[...]] + [get_pair(r, more) for r in late[1:]])


def join_shares(early, late, small, after):
    rows, width = early[0].shape
    return small_launch(
        partial(join_kernel, len(early)),
        "join_shares",
        (*early, *late, small),
        [shaped((rows + late[0].shape[0], width), BF16), shaped((SMALL, width), F32)],
        after=after,
    )


def lay_kernel(slot, where, *refs):
    parts, (small, other, out) = refs[:-3], refs[-3:]
    rows = parts[0].shape[0]
    for d, ref in enumerate(parts):
        out[pl.ds(pl.multiple_of((where[slot] ^ d) * rows, rows), rows), :] = ref[...]
    put_pair(out, len(parts) * rows, small[...] + other[...])


def along(value, d):
    return swap(value, (0, 4 * d))


def spread(pieces, send):
    return [pieces[0]] + [send(piece, d) for d, piece in enumerate(pieces) if d > 0]


def gather_along(where, share, small, after):
    rows, width = share.shape
    parts = spread([share] * ALONG, along)
    return small_launch(
        partial(lay_kernel, 3),
        "lay",
        (where, *parts, small, swap(small, (0, 1))),
        [shaped((ALONG * rows + 2 * SMALL, width), BF16)],
        after=after,
    )[0]


def halve_kernel(across, along_row, low, high):
    low[...] = across[0 : low.shape[0], :]
    high[...] = along_row[low.shape[0] :, :]


def collect_kernel(own, across, along_row, low, high, out, small):
    rows, cut = out.shape[1], low.shape[0]
    out[0] = along_row[0:rows, :]
    out[1] = across[0:rows, :]
    out[2, 0:cut, :] = low[...]
    out[2, cut:rows, :] = high[0 : rows - cut, :]
    far = get_pair(high, rows - cut)
    small[...] = (get_pair(own, rows) + get_pair(along_row, rows)) + (get_pair(across, rows) + far)


def gather_plane(quarter, after):
    theirs = swap(quarter, (0, 1))
    rows, width = quarter.shape
    across, along_row = in_plane(quarter, 2), in_plane(quarter, 1)
    cut = rows // 32 * 16
    low, high = small_launch(
        halve_kernel, "halve", (across, along_row), [shaped((cut, width), BF16), shaped((rows - cut, width), BF16)],
        after=after,
    )
    mine, small = small_launch(
        collect_kernel,
        "collect",
        (quarter, across, along_row, in_plane(low, 1), in_plane(high, 2)),
        [shaped((PLANE - 1, rows - 2 * SMALL, width), BF16), shaped((SMALL, width), F32)],
    )
    return small, (quarter, mine), (theirs, swap(mine, (0, 1)))


def unpack_kernel(flip, early, where, first, rest, o_w1, o_w2, o_qkv, o_proj, feed_buf, att_buf, sems):
    me, side = where[2], where[1] ^ flip
    width = o_proj.shape[0]
    late = width // 2 // ALONG
    low, high = slice(0, width // 2), slice(width // 2, width)
    def quarter_of(d):
        return first if d == 0 else rest.at[d - 1]

    def place(d):
        return pl.ds(pl.multiple_of((me ^ d) * width, width), width)

    for d in range(PLANE):
        for share in range(ALONG):
            start = share * (early + late) + early
            att_buf[me ^ d, share * late : (share + 1) * late, :] = quarter_of(d)[start : start + late, :].astype(F32)

    def run(att_targets, feed_target, turned):
        copies = []
        for index, (target, rows, cols) in enumerate(att_targets):
            copies.append(pltpu.make_async_copy(att_buf.at[index], target.at[rows, cols], sems.at[len(copies)]))
            copies[-1].start()
        for d in range(PLANE):
            shares = [quarter_of(d)[i * (early + late) : i * (early + late) + early, :] for i in range(ALONG)]
            block = jnp.concatenate(shares, axis=0).astype(F32)
            feed_buf[d] = block.T if turned else block
            copies.append(pltpu.make_async_copy(feed_buf.at[d], feed_target(d), sems.at[len(copies)]))
            copies[-1].start()
        for copy in copies:
            copy.wait()

    def halves(target, cols):
        return [(target, low, cols), (target, high, cols)]

    @pl.when(side == 0)
    def _():
        targets = halves(o_qkv, slice(0, width)) + halves(o_qkv, slice(width, 2 * width))
        run(targets, lambda d: o_w1.at[:, place(d)], False)

    @pl.when(side == 1)
    def _():
        targets = halves(o_qkv, slice(2 * width, 3 * width)) + halves(o_proj, slice(0, width))
        run(targets, lambda d: o_w2.at[place(d), :], True)


def unpack(flip, early, where, half, shapes, so_far):
    width = half[0].shape[1]
    vector = pl.BlockSpec(memory_space=pltpu.VMEM)
    return launch(
        partial(unpack_kernel, flip, early),
        "unpack",
        (),
        (where, *half),
        [pl.BlockSpec(memory_space=pltpu.SMEM), vector, vector],
        [shaped(shape, F32) for shape in shapes],
        [pl.BlockSpec(memory_space=pl.ANY)] * len(shapes),
        so_far=so_far,
        scratch=[
            pltpu.VMEM((PLANE, width, width), F32),
            pltpu.VMEM((PLANE, width // 2, width), F32),
            pltpu.SemaphoreType.DMA((2 * PLANE,)),
        ],
        vmem=24,
    )


def body(images, cotangent, norm1_gain, norm1_shift, qkv_weight, qv_bias, proj_weight, proj_bias, *rest):
    pos = rest[:13]
    norm2_gain, norm2_shift, fc1_weight, fc1_bias, fc2_weight, fc2_bias = rest[13:]
    total, _, cols, width = images.shape
    hidden = fc1_weight.shape[1]
    per_step = 4
    band, batch = lax.axis_index("band"), lax.axis_index("batch")
    where = jnp.stack([band, batch % 2, band * 2 + batch // 2 % 2, batch // 4 % ALONG]).astype(jnp.int32)
    head_of_row = np.arange(STACK)[:, None] // TOKENS
    mask = jnp.asarray(head_of_row == np.arange(LANES)[None, :] // HEAD_DIM, BF16)
    to_partner = lambda value: swap(value, (1, 0))
    pos = (*pos[:12], pos[12].T)

    later = (total // per_step * 2 // 5) * per_step
    image_chunks = [(0, later), (later, total - later)]
    packed, token = pack_rows((images,), [(0, *image_chunks[0])])
    received = to_partner(packed)
    later_packed, cot_packed, _ = pack_rows(
        (images, cotangent), [(0, *image_chunks[1]), (1, 0, total)], (token,)
    )
    pair, later_packed, cot_packed = pair_bias(pos, (later_packed, cot_packed))
    later_received = to_partner(later_packed)
    norm_one = (norm1_gain, norm1_shift, qkv_weight, qv_bias, pair, mask)
    so_far = attend(where, images, received, 0, per_step, *norm_one, (), ())
    _, cot_packed = small_launch(
        token_kernel, "order", (), [TOKEN], after=(*so_far[:1], later_received), vmem=60, through=(cot_packed,)
    )
    cot_rows = to_partner(cot_packed)
    so_far = attend(where, images, later_received, later, per_step, *norm_one, so_far, ())
    x, normed, qkv, probs, att = so_far
    weights = (proj_weight, proj_bias, norm2_gain, norm2_shift, fc1_weight, fc1_bias, fc2_weight, fc2_bias)
    result = feed(where, cotangent, cot_rows, per_step, x, att, weights)
    out_images, grad_mid, grad_att, out_sent, feed_small, feed_b1, mine, theirs, grad_proj = result
    out_rows = to_partner(out_sent)
    flat = lambda value: value.reshape(-1, width)
    early = [flat(mine), swap(flat(theirs), (0, 1))]

    saved = (normed, qkv, probs, grad_att)
    grads, att_small, grad_pair, mine, theirs = attend_back(
        where, 0, total, per_step, saved, mask, grad_proj, None, (), True, ()
    )
    *pieces, token = split_share(where, 2, PLANE, early, (out_rows, att_small), 5e9)
    early = spread(pieces, in_plane)
    *pieces, token = split_share(where, 2, PLANE, [flat(mine), swap(flat(theirs), (0, 1))], (token,))
    late = spread(pieces, in_plane)
    grad_images, sent, norm_small = image_grads(where, 0, total, per_step, grads, x, grad_mid, norm1_gain,
                                                qkv_weight, images.shape, (), (), (token,))
    grad_rows = to_partner(sent)
    small = gather_small(feed_small, feed_b1, att_small, norm_small, grad_pair)
    *pieces, token = split_share(where, 3, ALONG, early, (small,))
    early = spread(pieces, along)
    *pieces, small, _ = split_with_small(where, 3, ALONG, late, [small], (token,))
    late = spread(pieces, along)
    share, small = join_shares(early, late, small, ())
    stride = PLANE * ALONG
    while stride < lax.axis_size("batch"):
        share = (share.astype(F32) + swap(share, (0, stride)).astype(F32)).astype(BF16)
        small = small + swap(small, (0, stride))
        stride *= 2
    out_images, token = merge_rows(out_rows, out_images, 0)
    quarter = gather_along(where, share, small, (token,))
    grad_images, token = merge_rows(grad_rows, grad_images, 0)
    small, half, other_half = gather_plane(quarter, (token,))
    smalls = finish_small(pos, small, hidden)
    shapes = [w.shape for w in (fc1_weight, fc2_weight, qkv_weight, proj_weight)]
    large = unpack(0, early[0].shape[0], where, half, shapes, ())
    grad_fc1, grad_fc2, grad_qkv, grad_proj = unpack(1, early[0].shape[0], where, other_half, shapes, large)
    n1_gain, n1_shift, qv, proj_b, n2_gain, n2_shift, fc1_b, fc2_b = smalls[:8]
    return (out_images, grad_images, n1_gain, n1_shift, grad_qkv, qv, grad_proj, proj_b, *smalls[8:20], smalls[20].T,
            n2_gain, n2_shift, grad_fc1, fc1_b, grad_fc2, fc2_b)


def solution(mesh):
    tokens = P("batch", "band", None, None)
    return jax.shard_map(
        body,
        mesh=mesh,
        in_specs=(tokens, tokens) + (P(),) * 25,
        out_specs=(tokens, tokens) + (P(),) * 25,
        check_vma=False,
    )
```
